32 devices in a mesh: space: 8 (over z, core), chaos: 4 (over y, x).
Axes of the slice: x: 2, y: 2, z: 4, core: 2. Of those that a mesh axis runs over, the one named last changes fastest.
Arguments:
- chaos_modes: float32 [84, 32768], P(None, ('space', 'chaos')), may hold values from -0.2 to 0.2
- newton_heading: float32 [84, 32768], P(None, ('space', 'chaos')), may hold values from -0.2 to 0.2
- source: float32 [32768], P(('space', 'chaos')), may hold values from -6 to 6
- nodes: float32 [512, 6], replicated, may hold values from -3 to 3
- weights: float32 [512], replicated, may hold values from 0.0009765625 to 0.0029296875
- k_ref: float32 [4], replicated, may hold values from 0.5 to 4
- sensitivity: float32 [4, 6], replicated, may hold values from -0.1 to 0.1
- decay: float32 [4], replicated, may hold values from 0.1 to 0.5
- material: int32 [512], P('space'), may hold values from 0 to 3
- neighbors: int32 [512, 4], P('space'), may hold values from -1 to 79, as said below
- send_list: int32 [8, 8, 2], P('space'), may hold values from 0 to 63, as said below
Outputs:
- residual: float32 [84, 32768], P(None, ('space', 'chaos'))
- jvp_out: float32 [84, 32768], P(None, ('space', 'chaos'))
The draws below stay inside these ranges and needn't reach their ends.
Inputs may be any that keep to these rules, and one draw needn't show every extreme that they name: `neighbors`: -1 marks a face without neighbour. An entry below 64 is a block of the same partition; an entry 64 + t * 2 + j names slot j of what partition t sends here, where t is one or two indices away along space, cyclically, and the slot is live. send_list[s, t, j] is a local block of partition s. Only slots named by some neighbour entry are live: from s to a partition one or two indices away, cyclically, between 1 and 2 leading slots; to any other partition none.
All inputs are finite; a program needn't handle non-finite values.
Results may differ from the reference program's by a relative error of at most 0.0003.
Values sent between devices are 32-bit elements; how exact they have to be, the bound alone decides.
A program may use at most 192 MiB of HBM per device.

```python
import math
import jax
import jax.numpy as jnp
import numpy as np
from jax import lax

DIMS = 6
P_SIZE = 84
NMAT = 4
SEGMENT_SITES = 64
GAUSS_POINTS = 128
HMAX = 2
NB = 64
Q = 512
CELLS = 32768
N_SPACE = 8
N_CHAOS = 4


def halo_counts(key):
    count_key = jax.random.fold_in(key, 7)
    first_key, second_key = jax.random.split(count_key)
    sender = jnp.arange(N_SPACE, dtype=jnp.int32)[:, None]
    receiver = jnp.arange(N_SPACE, dtype=jnp.int32)[None, :]
    forward = (receiver - sender) % N_SPACE
    backward = (sender - receiver) % N_SPACE
    nearby = (forward == 1) | (forward == 2) | (backward == 1) | (backward == 2)
    counts = jax.random.randint(first_key, (N_SPACE, N_SPACE), 1, HMAX + 1, dtype=jnp.int32)
    chosen = jax.random.randint(second_key, (), 0, N_SPACE, dtype=jnp.int32)
    counts = jnp.where((sender == chosen) & (receiver == (chosen + 1) % N_SPACE), HMAX, counts)
    counts = jnp.where((sender == N_SPACE - 1) & (receiver == 0), HMAX, counts)
    return jnp.where(nearby, counts, 0)


def draw_send_list(key, part):
    return jax.random.randint(jax.random.fold_in(key, 11), (N_SPACE, N_SPACE, HMAX), 0, NB, dtype=jnp.int32)


def draw_neighbors(key, part):
    counts = halo_counts(key)
    local_key = jax.random.fold_in(key, 13)
    boundary_key = jax.random.fold_in(key, 17)
    block_ids = jnp.arange(NB, dtype=jnp.int32)[None, :, None]
    offsets = jax.random.randint(local_key, (N_SPACE, NB, 4), 1, NB, dtype=jnp.int32)
    local_ref = (block_ids + offsets) % NB
    boundary = jax.random.randint(boundary_key, (N_SPACE, NB, 4), 0, 8, dtype=jnp.int32) == 0
    local_ref = jnp.where(boundary, -1, local_ref)
    owner_rank = jnp.arange(N_SPACE, dtype=jnp.int32)[:, None]
    blocks = jnp.arange(NB, dtype=jnp.int32)[None, :]
    group_index = jnp.minimum(blocks // HMAX, 3)
    slot_index = blocks % HMAX
    stride = jnp.where(group_index == 0, -1, jnp.where(group_index == 1, 1, jnp.where(group_index == 2, -2, 2)))
    peer_rank = (owner_rank + stride) % N_SPACE
    live = (blocks < 4 * HMAX) & (slot_index < counts[peer_rank, owner_rank])
    halo_ref = NB + peer_rank * HMAX + slot_index
    face_three = jnp.where(live, halo_ref, local_ref[:, :, 3])
    result = local_ref.at[:, :, 3].set(face_three)
    return result.reshape(N_SPACE * NB, 4)


def place_ends(entries, own_key, least, largest):
    spot = [jax.random.randint(jax.random.fold_in(own_key, axis), (), 0, length) for axis, length in enumerate(entries.shape)]
    longest = entries.shape.index(max(entries.shape))
    next_to = spot[:longest] + [(spot[longest] + 1) % entries.shape[longest]] + spot[longest + 1:]
    return entries.at[tuple(spot)].set(least).at[tuple(next_to)].set(largest)


def block_levels(own_key, shape, pieces, least, top_value):
    def one(position, parts):
        draws = jax.random.uniform(jax.random.fold_in(jax.random.fold_in(own_key, 6), position), (parts,), jnp.float32, least / len(pieces), top_value / len(pieces))
        return jnp.repeat(jnp.exp(draws), shape[position] // parts).reshape((-1,) + (1,) * (len(shape) - position - 1))

    loudness = one(*pieces[0])
    for cut in pieces[1:]:
        loudness = loudness * one(*cut)
    return loudness


def noise(rng, extent, width, most, cuts=(), kind=jnp.bfloat16):
    values = width * jax.random.normal(rng, extent, jnp.float32)
    if cuts:
        values = values * block_levels(rng, extent, cuts, -0.22, 0.18)
    return jnp.clip(values, -most, most).astype(kind)


def setup_inputs(seed: int = 0) -> dict:
    seeds = jax.random.split(jax.random.key(seed), 12)
    chaos_modes = jnp.clip(jax.random.uniform(seeds[0], (P_SIZE, CELLS), jnp.float32, -0.2, 0.2) * block_levels(seeds[0], (P_SIZE, CELLS), ((1, 32),), -0.4, 0.0), -0.2, 0.2)
    newton_heading = jnp.clip(jax.random.uniform(seeds[1], (P_SIZE, CELLS), jnp.float32, -0.2, 0.2) * block_levels(seeds[1], (P_SIZE, CELLS), ((1, 32),), -0.4, 0.0), -0.2, 0.2)
    source = noise(seeds[2], (CELLS,), 1.0, 6.0, ((0, 32),), jnp.float32)
    nodes = noise(seeds[3], (Q, DIMS), 1.0, 3.0, (), jnp.float32)
    weights = jnp.clip(jax.random.uniform(seeds[4], (Q,), jnp.float32, 0.0009765625, 0.0029296875), 0.0009765625, 0.0029296875)
    k_ref = jnp.clip(jnp.exp(jax.random.uniform(seeds[5], (NMAT,), jnp.float32, math.log(0.5), math.log(4.0))), 0.5, 4.0)
    sensitivity = jnp.clip(jax.random.uniform(seeds[6], (NMAT, DIMS), jnp.float32, -0.1, 0.1), -0.1, 0.1)
    decay = jnp.clip(jnp.exp(jax.random.uniform(seeds[7], (NMAT,), jnp.float32, math.log(0.1), math.log(0.5))), 0.1, 0.5)
    material = place_ends(jax.random.randint(seeds[8], (N_SPACE * NB,), 0, NMAT), jax.random.fold_in(seeds[8], 1), 0, NMAT - 1).astype(jnp.int32)
    neighbors = draw_neighbors(jax.random.fold_in(seeds[11], 71), 0)
    send_list = draw_send_list(jax.random.fold_in(seeds[11], 71), 0)
    return dict(chaos_modes=chaos_modes, newton_heading=newton_heading, source=source, nodes=nodes, weights=weights, k_ref=k_ref, sensitivity=sensitivity, decay=decay, material=material, neighbors=neighbors, send_list=send_list)


lateral_factor = 0.5
cooler_multiplier = 2.0

def compositions(remaining, places):
    if places == 1:
        return [[remaining]]
    listing = []
    for leading in range(remaining, -1, -1):
        for trailing in compositions(remaining - leading, places - 1):
            listing.append([leading] + trailing)
    return listing

def chaos_orders(variables):
    listing = []
    for degree in range(4):
        listing = listing + compositions(degree, variables)
    return np.array(listing, dtype=np.int32)

def hermite_basis(points):
    polynomial_orders = chaos_orders(points.shape[1])
    scale_factors = np.array([1.0, 1.0, 1.0 / math.sqrt(2.0), 1.0 / math.sqrt(6.0)], dtype=np.float32)
    result = jnp.ones((points.shape[0], polynomial_orders.shape[0]), jnp.float32)
    for random_variable in range(points.shape[1]):
        column = points[:, random_variable]
        hermite = jnp.stack([jnp.ones_like(column), column, column * column - 1.0, column * column * column - 3.0 * column], axis=1)
        selection_mask = np.zeros((4, polynomial_orders.shape[0]), np.float32)
        selection_mask[polynomial_orders[:, random_variable], np.arange(polynomial_orders.shape[0])] = scale_factors[polynomial_orders[:, random_variable]]
        result = result * jnp.dot(hermite, jnp.asarray(selection_mask, dtype=jnp.float32), precision=lax.Precision.HIGHEST)
    return result

def pointwise_imbalance(site_kelvin, kelvin_linearized, diffusive_ability, admittance_linearized, interface_partner_slot):
    interface_transfer = 0.5 * (diffusive_ability[:, :, :-1] + diffusive_ability[:, :, 1:])
    interface_increment = 0.5 * (admittance_linearized[:, :, :-1] + admittance_linearized[:, :, 1:])
    kelvin_gap = site_kelvin[:, :, :-1] - site_kelvin[:, :, 1:]
    decline_increment = kelvin_linearized[:, :, :-1] - kelvin_linearized[:, :, 1:]
    heightwise_stream = interface_transfer * kelvin_gap
    stream_increment = interface_increment * kelvin_gap + interface_transfer * decline_increment
    padding_sheet = jnp.zeros(site_kelvin.shape[:2] + (1,), jnp.float32)
    energy_imbalance = jnp.concatenate([heightwise_stream, padding_sheet], 2) - jnp.concatenate([padding_sheet, heightwise_stream], 2)
    imbalance_linearized = jnp.concatenate([stream_increment, padding_sheet], 2) - jnp.concatenate([padding_sheet, stream_increment], 2)
    cooler_outflow = cooler_multiplier * diffusive_ability[:, :, :1] * site_kelvin[:, :, :1]
    cooler_linearized = cooler_multiplier * (admittance_linearized[:, :, :1] * site_kelvin[:, :, :1] + diffusive_ability[:, :, :1] * kelvin_linearized[:, :, :1])
    top_padding_sheet = jnp.zeros(site_kelvin.shape[:2] + (site_kelvin.shape[2] - 1,), jnp.float32)
    energy_imbalance = energy_imbalance + jnp.concatenate([cooler_outflow, top_padding_sheet], 2)
    imbalance_linearized = imbalance_linearized + jnp.concatenate([cooler_linearized, top_padding_sheet], 2)
    piled_vertical_lines = jnp.stack([site_kelvin, kelvin_linearized, diffusive_ability, admittance_linearized])
    for face_number in range(4):
        face_index = interface_partner_slot[:, face_number]
        present = (face_index >= 0).astype(jnp.float32)[None, :, None]
        bordering_sites = jnp.take(piled_vertical_lines, jnp.maximum(face_index, 0), axis=2)
        side_conduct = lateral_factor * 0.5 * (diffusive_ability + bordering_sites[2]) * present
        side_step = lateral_factor * 0.5 * (admittance_linearized + bordering_sites[3]) * present
        sideways_gap = site_kelvin - bordering_sites[0]
        flank_decline_increment = kelvin_linearized - bordering_sites[1]
        energy_imbalance = energy_imbalance + side_conduct * sideways_gap
        imbalance_linearized = imbalance_linearized + side_step * sideways_gap + side_conduct * flank_decline_increment
    return (energy_imbalance, imbalance_linearized)

def reference(chaos_modes, newton_heading, source, nodes, weights, k_ref, sensitivity, decay, material, neighbors, send_list):
    basis = hermite_basis(nodes)
    segment_aggregate = N_SPACE * NB
    owner_rank = jnp.arange(segment_aggregate, dtype=jnp.int32) // NB
    halo_ref = neighbors - NB
    peer_rank = jnp.clip(halo_ref // HMAX, 0, N_SPACE - 1).astype(jnp.int32)
    slot_index = jnp.clip(halo_ref % HMAX, 0, HMAX - 1).astype(jnp.int32)
    remote = send_list[peer_rank, owner_rank[:, None], slot_index]
    interface_partner_slot = jnp.where(neighbors < 0, -1, jnp.where(neighbors < NB, owner_rank[:, None] * NB + neighbors, peer_rank * NB + remote)).astype(jnp.int32)
    group_basis = basis.reshape(N_CHAOS, GAUSS_POINTS, basis.shape[1])
    group_weight = weights.reshape(N_CHAOS, GAUSS_POINTS)
    group_nodes = nodes.reshape(N_CHAOS, GAUSS_POINTS, nodes.shape[1])
    segment_damping = decay[material]

    def accumulate(totals, inputs):
        hermite_subset_evals, part_weight, part_nodes = inputs
        material_scale = k_ref[:, None] * jnp.exp(jnp.dot(sensitivity, part_nodes.T, precision=lax.Precision.HIGHEST))
        segment_multiplier = material_scale[material].T
        site_kelvin = jnp.dot(hermite_subset_evals, chaos_modes, precision=lax.Precision.HIGHEST).reshape(GAUSS_POINTS, segment_aggregate, SEGMENT_SITES)
        kelvin_linearized = jnp.dot(hermite_subset_evals, newton_heading, precision=lax.Precision.HIGHEST).reshape(GAUSS_POINTS, segment_aggregate, SEGMENT_SITES)
        diffusive_ability = segment_multiplier[:, :, None] * jnp.exp(-segment_damping[None, :, None] * site_kelvin)
        admittance_linearized = -segment_damping[None, :, None] * diffusive_ability * kelvin_linearized
        energy_imbalance, imbalance_linearized = pointwise_imbalance(site_kelvin, kelvin_linearized, diffusive_ability, admittance_linearized, interface_partner_slot)
        weighted = (energy_imbalance * part_weight[:, None, None]).reshape(GAUSS_POINTS, segment_aggregate * SEGMENT_SITES)
        weighted_step = (imbalance_linearized * part_weight[:, None, None]).reshape(GAUSS_POINTS, segment_aggregate * SEGMENT_SITES)
        first = totals[0] + jnp.dot(hermite_subset_evals.T, weighted, precision=lax.Precision.HIGHEST)
        second = totals[1] + jnp.dot(hermite_subset_evals.T, weighted_step, precision=lax.Precision.HIGHEST)
        return ((first, second), None)
    start = jnp.zeros(chaos_modes.shape, jnp.float32)
    (projected, projected_step), unused = lax.scan(accumulate, (start, start), (group_basis, group_weight, group_nodes))
    node_mass = jnp.dot(weights, basis, precision=lax.Precision.HIGHEST)
    residual = projected - node_mass[:, None] * source[None, :]
    return (residual, projected_step)
```

```python
import functools
import math

import jax
import jax.numpy as jnp
import numpy as np
from jax import lax
from jax.experimental import pallas as pl
from jax.experimental.pallas import tpu as pltpu
from jax.sharding import PartitionSpec as P

NMAT = 4
SITES = 64
TERMS = 84
MAIN = 80
LOG2E = 1.0 / math.log(2.0)
LN2 = math.log(2.0)
OFFSETS = (1, -1, 2, -2)
SPAN = 512
BF = jnp.bfloat16
F32 = jnp.float32


def compositions(remaining, places):
    if places == 1:
        return [[remaining]]
    listing = []
    for leading in range(remaining, -1, -1):
        for trailing in compositions(remaining - leading, places - 1):
            listing.append([leading] + trailing)
    return listing


def chaos_orders(variables):
    listing = []
    for degree in range(4):
        listing = listing + compositions(degree, variables)
    return np.array(listing, dtype=np.int32)


def half_turn(x, wanted):
    return jnp.where(wanted, pltpu.roll(x, 64, 1), x)


def factors(x, o):
    second = (x * x - 1.0) * np.float32(1.0 / math.sqrt(2.0))
    third = (x * x * x - 3.0 * x) * np.float32(1.0 / math.sqrt(6.0))
    return jnp.where(o == 0, 1.0, jnp.where(o == 1, x, jnp.where(o == 2, second, third)))


def order_codes(dims):
    orders = chaos_orders(dims)
    code = (orders * 4 ** np.arange(dims)[None, :]).sum(1)
    out = np.zeros((8, 128), np.float32)
    out[0, :TERMS] = code
    return out


def upright(row):
    return jnp.transpose(jnp.broadcast_to(row, (128, 128)))


def stacked(main, tail, lower):
    row = lax.broadcasted_iota(jnp.int32, tail.shape, 0)
    high = main.astype(BF)
    low = (main - high.astype(F32)).astype(BF)
    tail_high = tail.astype(BF).astype(F32)
    tail_low = tail - tail_high
    if lower:
        parts = [high, high, low]
        ends = [jnp.where(row < 4, tail_high, pltpu.roll(tail_high, 4, 0)), tail_low]
    else:
        parts = [high, low, high]
        ends = [jnp.where(row < 4, tail_high, pltpu.roll(tail_low, 4, 0)), tail_high]
    ends[1] = jnp.where(row < 4, ends[1], 0.0)
    return jnp.concatenate(parts + [jnp.concatenate(ends, 0).astype(BF)], 0)


def fill_tables(nodes_t, weights, codes, left, right, mass):
    dims = nodes_t.shape[0]
    code = upright(codes[0:1, 0:128])[0:88].astype(jnp.int32)
    row = lax.broadcasted_iota(jnp.int32, (88, 1), 0)
    mass[...] = jnp.zeros(mass.shape, F32)

    def body(part, carry):
        span = pl.ds(pl.multiple_of(part * 128, 128), 128)
        value = jnp.ones((88, 128), F32)
        for d in range(dims):
            value = value * factors(nodes_t[d : d + 1, span], (code // 4**d) % 4)
        value = jnp.where(row < TERMS, value, 0.0)
        left[:, span] = stacked(value[0:80], value[80:88], True)
        value = value * weights[:, span]
        mass[...] += jnp.sum(value, axis=1, keepdims=True)
        value = value * 0.25
        high = value.astype(BF).astype(F32)
        right[:, span] = jnp.concatenate([high, value - high], 0).astype(BF)
        return carry

    lax.fori_loop(0, nodes_t.shape[1] // 128, body, 0)


def fill_aux(k_ref, sensitivity, decay, material, table, field):
    row = lax.broadcasted_iota(jnp.int32, (8, 128), 0)
    low_half = lax.broadcasted_iota(jnp.int32, (8, 128), 1) < 64
    dims = sensitivity.shape[1]
    for m in range(NMAT):
        tile = jnp.log(jnp.full((8, 128), k_ref[m], F32))
        for d in range(dims):
            tile = jnp.where(row == d + 1, sensitivity[m, d], tile)
        tile = jnp.where(row == 7, -decay[m], tile) * np.float32(LOG2E)
        table[m, 0] = pltpu.roll(tile, 4, 0)
        table[m, 1] = tile
    for i in range(material.shape[0] // 2):
        a, b = material[2 * i], material[2 * i + 1]
        for f in range(2):
            field[i, f, 84:88] = jnp.where(low_half, table[a, f], table[b, f])[4:8]


def remote(src, dst, send, recv, device):
    return pltpu.make_async_remote_copy(
        src_ref=src, dst_ref=dst, send_sem=send, recv_sem=recv,
        device_id=device, device_id_type=pl.DeviceIdType.MESH,
    )


def greet(space_count, chaos_count, space, chaos):
    barrier = pltpu.get_barrier_semaphore()
    if chaos_count == 4:
        peers = [chaos + 1 - 2 * (chaos % 2), (chaos + 2) % 4]
    else:
        peers = [(chaos + k) % chaos_count for k in range(1, chaos_count)]
    for peer in peers:
        pl.semaphore_signal(
            barrier, inc=1, device_id={"chaos": peer}, device_id_type=pl.DeviceIdType.MESH
        )
    for offset in OFFSETS:
        pl.semaphore_signal(
            barrier, inc=1, device_id={"space": (space + offset + space_count) % space_count},
            device_id_type=pl.DeviceIdType.MESH,
        )
    return barrier, peers


def evaluate(m, h, index, basis, store):
    row = lax.broadcasted_iota(jnp.int32, (8, 128), 0)
    aux = jnp.where(row < 4, pltpu.roll(m[80:88], 4, 0), h[80:88])
    damp = aux[7:8]
    arg = m * damp
    first = arg[0:8] + jnp.where(row < 7, aux, 0.0)
    rate = jnp.transpose(jnp.broadcast_to(damp * np.float32(LN2), (128, 128)))
    sides = [
        jnp.transpose(stacked(x, y, False))
        for x, y in (
            (m[0:80], m[80:88]), (h[0:80], h[80:88]),
            (jnp.concatenate([first, arg[8:80]], 0), arg[80:88]),
        )
    ]
    rows = [s[16 * c : 16 * c + 16] for c in range(8) for s in sides]
    r = jnp.dot(jnp.concatenate(rows, 0), basis, preferred_element_type=F32)
    for c in range(8):
        t = r[48 * c : 48 * c + 16]
        dt = r[48 * c + 16 : 48 * c + 32]
        k = jnp.exp2(r[48 * c + 32 : 48 * c + 48])
        speed = rate[16 * c : 16 * c + 16]
        dk = k * (dt * jnp.concatenate([speed] * (dt.shape[1] // 128), 1))
        block = 2 * index + c // 4
        at = slice(16 * (c % 4), 16 * (c % 4) + 16)
        store[block, 0, at] = t
        store[block, 1, at] = dt
        store[block, 2, at] = k
        store[block, 3, at] = dk


def columns(block, index, store, acc):
    width = 128
    shape = (SITES, width)
    row = lax.broadcasted_iota(jnp.int32, shape, 0)
    top = row == SITES - 1
    bottom = row == 0
    for part in range(store.shape[3] // width):
        at = slice(part * width, part * width + width)
        t, dt, k, dk = [store[block, f, :, at] for f in range(4)]
        up = [pltpu.roll(x, SITES - 1, 0) for x in (t, dt, k, dk)]
        gap = jnp.where(top, 0.0, t - up[0])
        step = jnp.where(top, 0.0, dt - up[1])
        both = k + up[2]
        change = dk + up[3]
        flow = both * gap
        turn = change * gap + both * step
        below = jnp.where(bottom, -4.0 * k * t, pltpu.roll(flow, 1, 0))
        under = jnp.where(bottom, -4.0 * (k * dt + dk * t), pltpu.roll(turn, 1, 0))
        acc[index, 0, :, at] = 2.0 * (flow - below)
        acc[index, 1, :, at] = 2.0 * (turn - under)


def send_halo(space_count, space, picks, field, out, inbox, send, recv):
    low_half = lax.broadcasted_iota(jnp.int32, (1, 128), 1) < 64
    copies = []
    for i, offset in enumerate(OFFSETS):
        target = (space + offset + space_count) % space_count
        e0 = picks[2 * target]
        e1 = picks[2 * target + 1]
        for f in range(2):
            x0 = half_turn(field[e0 // 2, f], e0 % 2 == 1)
            x1 = half_turn(field[e1 // 2, f], e1 % 2 == 0)
            out[i, f] = jnp.where(low_half, x0, x1)
        copy = remote(out.at[i], inbox.at[i], send.at[i], recv.at[i], {"space": target})
        copy.start()
        copies.append(copy)
    return copies


def slot(neighbors, own, block, face, ranks, halo_depth):
    space, space_count, blocks = ranks
    entry = neighbors[face, block]
    away = jnp.maximum(entry - blocks, 0)
    distance = (space - away // halo_depth + space_count) % space_count
    order = jnp.where(
        distance == 1, 0, jnp.where(distance == space_count - 1, 1, jnp.where(distance == 2, 2, 3))
    )
    index = jnp.where(
        entry >= blocks, blocks + order * halo_depth + away % halo_depth, entry
    )
    return jnp.where(entry >= 0, index, own)


def faces(pair, base, ranks, halo_depth, neighbors, store, acc, bal):
    for j in range(2):
        own = 2 * (base + pair) + j
        mine = 2 * pair + j
        others = [slot(neighbors, own, own, f, ranks, halo_depth) for f in range(4)]
        for c in range(SITES // 16):
            rows = slice(16 * c, 16 * c + 16)
            for part in range(store.shape[3] // 256):
                at = slice(part * 256, part * 256 + 256)
                t, dt, k, dk = [store[own, f, rows, at] for f in range(4)]
                flow = acc[mine, 0, rows, at]
                turn = acc[mine, 1, rows, at]
                for e in others:
                    gap = t - store[e, 0, rows, at]
                    step = dt - store[e, 1, rows, at]
                    both = k + store[e, 2, rows, at]
                    change = dk + store[e, 3, rows, at]
                    flow += both * gap
                    turn += change * gap + both * step
                for side, x in ((0, flow), (1, turn)):
                    high = x.astype(BF)
                    spot = slice(128 * side + 64 * j + 16 * c, 128 * side + 64 * j + 16 * c + 16)
                    bal[0, spot, at] = high
                    bal[1, spot, at] = (x - high.astype(F32)).astype(BF)


def project(pair, nodes_at, first, right, bal, mass, source, res, jvp):
    turned = (((1,), (1,)), ((), ()))
    one = lax.dot_general(right[:, nodes_at], bal[0], turned, preferred_element_type=F32)
    two = lax.dot_general(right[0:88, nodes_at], bal[1], turned, preferred_element_type=F32)
    total = one[0:88] + one[88:176] + two
    cols = pl.ds(pl.multiple_of(pair * 128, 128), 128)
    if first:
        res[:, cols] = (total[:, 0:128] - mass[...] * source[:, cols])[0:TERMS]
        jvp[:, cols] = total[0:TERMS, 128:256]
    else:
        res[:, cols] += total[0:TERMS, 0:128]
        jvp[:, cols] += total[0:TERMS, 128:256]


def whole_kernel(
    sizes, picks, k_ref, sensitivity, decay, material, neighbors, modes_far, heading_far,
    nodes_far, weights_far, codes_far, source, res, jvp,
    field, left, right, mass, store, acc, bal,
    nodes_t, weights, codes, table, out, inbox,
    send, recv, halo_send, halo_recv, near, local,
):
    space_count, chaos_count, pairs, halo_depth = sizes
    space = lax.axis_index("space")
    chaos = lax.axis_index("chaos")
    blocks = material.shape[0]
    base = chaos * pairs
    ranks = (space, space_count, blocks)
    barrier, peers = greet(space_count, chaos_count, space, chaos)
    loads = [
        pltpu.make_async_copy(
            far.at[:, i * 128 : i * 128 + 128], field.at[base + i, f, 0:TERMS],
            local.at[2 * i + f],
        )
        for i in range(pairs)
        for f, far in enumerate((modes_far, heading_far))
    ]
    extras = [
        pltpu.make_async_copy(a, b, near.at[i])
        for i, (a, b) in enumerate(
            [(nodes_far, nodes_t), (weights_far, weights), (codes_far, codes)]
        )
    ]
    for load in loads + extras:
        load.start()
    for load in loads:
        load.wait()
    pl.semaphore_wait(barrier, len(peers) + len(OFFSETS))

    def block(owner, first, count):
        return field.at[pl.ds(owner * pairs + first, count), :, 0:TERMS]

    def passing(i, owner, first, count, target):
        ref = block(owner, first, count)
        return remote(ref, ref, send.at[i], recv.at[i], {"chaos": target})

    width = store.shape[3]

    def evaluate_span(start, count, nodes_at=slice(0, width)):
        def body(i, carry):
            evaluate(
                field[start + i, 0], field[start + i, 1], start + i, left[:, nodes_at], store
            )
            return carry

        lax.fori_loop(0, count, body, 0)

    def own_columns():
        def body(i, carry):
            columns(2 * base + i, i, store, acc)
            return carry

        lax.fori_loop(0, 2 * pairs, body, 0)

    def finish(nodes_at, first):
        def late(pair, carry):
            faces(pair, base, ranks, halo_depth, neighbors, store, acc, bal)
            project(pair, nodes_at, first, right, bal, mass, source, res, jvp)
            return carry

        lax.fori_loop(0, pairs, late, 0)

    def mine():
        fill_aux(k_ref, sensitivity, decay, material, table, field)
        for load in extras:
            load.wait()
        fill_tables(nodes_t, weights, codes, left, right, mass)
        evaluate_span(base, pairs)
        own_columns()

    if chaos_count == 4:
        across, along = peers
        half = pairs // 2
        diagonal = 3 - chaos
        copies = [
            passing(0, chaos, 0, half, across), passing(1, chaos, half, half, along),
            passing(2, chaos, half, half, across), passing(3, chaos, 0, half, along),
        ]
        for copy in copies:
            copy.start()
        mine()
        copies[0].wait_recv()
        on = passing(4, across, 0, half, along)
        on.start()
        copies[1].wait_recv()
        over = passing(5, along, half, half, across)
        over.start()
        evaluate_span(across * pairs, half)
        evaluate_span(along * pairs + half, half)
        copies[2].wait_recv()
        evaluate_span(across * pairs + half, half)
        copies[3].wait_recv()
        evaluate_span(along * pairs, half)
        on.wait_recv()
        over.wait_recv()
        copies = copies + [on, over]
        halo = send_halo(space_count, space, picks, field, out, inbox, halo_send, halo_recv)
        evaluate_span(diagonal * pairs, pairs)
    else:
        copies = [passing(i, chaos, 0, pairs, t) for i, t in enumerate(peers)]
        for copy in copies:
            copy.start()
        mine()
        for i, copy in enumerate(copies):
            copy.wait_recv()
        halo = send_halo(space_count, space, picks, field, out, inbox, halo_send, halo_recv)
        for i in range(1, chaos_count):
            evaluate_span(((chaos + i) % chaos_count) * pairs, pairs)
    for i, copy in enumerate(halo):
        copy.wait_recv()
        evaluate(inbox[i, 0], inbox[i, 1], blocks // 2 + i, left[:, 0:width], store)
    finish(slice(0, width), True)

    def again(part, carry):
        nodes_at = pl.ds(pl.multiple_of(part * width, width), width)
        evaluate_span(0, blocks // 2, nodes_at)
        for i in range(len(OFFSETS)):
            evaluate(inbox[i, 0], inbox[i, 1], blocks // 2 + i, left[:, nodes_at], store)
        own_columns()
        finish(nodes_at, False)
        return carry

    if left.shape[1] > width:
        lax.fori_loop(1, left.shape[1] // width, again, 0)
    for copy in copies + halo:
        copy.wait_send()


def per_device(
    chaos_modes, newton_heading, source, nodes, weights, k_ref, sensitivity, decay,
    material, neighbors, send_list,
):
    space_count = lax.axis_size("space")
    cells = chaos_modes.shape[1]
    pairs = cells // 128
    halo_depth = send_list.shape[2]
    queue = nodes.shape[0]
    span = min(queue, SPAN)
    blocks = material.shape[0]
    far = pl.BlockSpec(memory_space=pltpu.HBM)
    vmem = pl.BlockSpec(memory_space=pltpu.VMEM)
    smem = pl.BlockSpec(memory_space=pltpu.SMEM)
    return pl.pallas_call(
        functools.partial(
            whole_kernel, (space_count, lax.axis_size("chaos"), pairs, halo_depth)
        ),
        out_shape=[jax.ShapeDtypeStruct((TERMS, cells), F32)] * 2,
        in_specs=[smem] * 6 + [far] * 5 + [vmem],
        out_specs=[vmem] * 2,
        scratch_shapes=[
            pltpu.VMEM((blocks // 2, 2, 88, 128), F32),
            pltpu.VMEM((256, queue), BF),
            pltpu.VMEM((176, queue), BF),
            pltpu.VMEM((88, 1), F32),
            pltpu.VMEM((blocks + 8, 4, SITES, span), F32),
            pltpu.VMEM((2 * pairs, 2, SITES, span), F32),
            pltpu.VMEM((2, 256, span), BF),
            pltpu.VMEM((nodes.shape[1], queue), F32),
            pltpu.VMEM((1, queue), F32),
            pltpu.VMEM((8, 128), F32),
            pltpu.VMEM((NMAT, 2, 8, 128), F32),
            pltpu.VMEM((4, 2, 88, 128), F32),
            pltpu.VMEM((4, 2, 88, 128), F32),
            pltpu.SemaphoreType.DMA((16,)),
            pltpu.SemaphoreType.DMA((16,)),
            pltpu.SemaphoreType.DMA((4,)),
            pltpu.SemaphoreType.DMA((4,)),
            pltpu.SemaphoreType.DMA((3,)),
            pltpu.SemaphoreType.DMA((2 * pairs,)),
        ],
        compiler_params=pltpu.CompilerParams(
            collective_id=0, has_side_effects=True, vmem_limit_bytes=60 * 1024 * 1024
        ),
    )(
        send_list.reshape(-1), k_ref, sensitivity, decay, material, neighbors.T, chaos_modes,
        newton_heading, nodes.T, weights[None, :], jnp.asarray(order_codes(nodes.shape[1])),
        source[None, :],
    )


def solution(mesh):
    return jax.shard_map(
        per_device,
        mesh=mesh,
        in_specs=(
            P(None, ("space", "chaos")),
            P(None, ("space", "chaos")),
            P(("space", "chaos")),
            P(), P(), P(), P(), P(),
            P("space"),
            P("space", None),
            P("space", None, None),
        ),
        out_specs=(P(None, ("space", "chaos")), P(None, ("space", "chaos"))),
        check_vma=False,
    )
```

```python
import functools
import math

import jax
import jax.numpy as jnp
import numpy as np
from jax import lax
from jax.experimental import pallas as pl
from jax.experimental.pallas import tpu as pltpu
from jax.sharding import PartitionSpec as P

NMAT = 4
SITES = 64
TERMS = 84
MAIN = 80
LOG2E = 1.0 / math.log(2.0)
LN2 = math.log(2.0)
OFFSETS = (1, -1, 2, -2)
SPAN = 512
BF = jnp.bfloat16
F32 = jnp.float32


def compositions(remaining, places):
    if places == 1:
        return [[remaining]]
    listing = []
    for leading in range(remaining, -1, -1):
        for trailing in compositions(remaining - leading, places - 1):
            listing.append([leading] + trailing)
    return listing


def chaos_orders(variables):
    listing = []
    for degree in range(4):
        listing = listing + compositions(degree, variables)
    return np.array(listing, dtype=np.int32)


def half_turn(x, wanted):
    return jnp.where(wanted, pltpu.roll(x, 64, 1), x)


def factors(x, o):
    second = (x * x - 1.0) * np.float32(1.0 / math.sqrt(2.0))
    third = (x * x * x - 3.0 * x) * np.float32(1.0 / math.sqrt(6.0))
    return jnp.where(o == 0, 1.0, jnp.where(o == 1, x, jnp.where(o == 2, second, third)))


def order_codes(dims):
    orders = chaos_orders(dims)
    code = (orders * 4 ** np.arange(dims)[None, :]).sum(1)
    out = np.zeros((8, 128), np.float32)
    out[0, :TERMS] = code
    return out


def upright(row):
    return jnp.transpose(jnp.broadcast_to(row, (128, 128)))


def stacked(main, tail, lower):
    row = lax.broadcasted_iota(jnp.int32, tail.shape, 0)
    high = main.astype(BF)
    low = (main - high.astype(F32)).astype(BF)
    tail_high = tail.astype(BF).astype(F32)
    tail_low = tail - tail_high
    if lower:
        parts = [high, high, low]
        ends = [jnp.where(row < 4, tail_high, pltpu.roll(tail_high, 4, 0)), tail_low]
    else:
        parts = [high, low, high]
        ends = [jnp.where(row < 4, tail_high, pltpu.roll(tail_low, 4, 0)), tail_high]
    ends[1] = jnp.where(row < 4, ends[1], 0.0)
    return jnp.concatenate(parts + [jnp.concatenate(ends, 0).astype(BF)], 0)


def fill_tables(nodes_t, weights, codes, left, right, mass):
    dims = nodes_t.shape[0]
    code = upright(codes[0:1, 0:128])[0:88].astype(jnp.int32)
    row = lax.broadcasted_iota(jnp.int32, (88, 1), 0)
    mass[...] = jnp.zeros(mass.shape, F32)

    def body(part, carry):
        span = pl.ds(pl.multiple_of(part * 128, 128), 128)
        value = jnp.ones((88, 128), F32)
        for d in range(dims):
            value = value * factors(nodes_t[d : d + 1, span], (code // 4**d) % 4)
        value = jnp.where(row < TERMS, value, 0.0)
        left[:, span] = stacked(value[0:80], value[80:88], True)
        value = value * weights[:, span]
        mass[...] += jnp.sum(value, axis=1, keepdims=True)
        value = value * 0.25
        high = value.astype(BF).astype(F32)
        right[:, span] = jnp.concatenate([high, value - high], 0).astype(BF)
        return carry

    lax.fori_loop(0, nodes_t.shape[1] // 128, body, 0)


def fill_aux(k_ref, sensitivity, decay, material, table, field):
    row = lax.broadcasted_iota(jnp.int32, (8, 128), 0)
    low_half = lax.broadcasted_iota(jnp.int32, (8, 128), 1) < 64
    dims = sensitivity.shape[1]
    for m in range(NMAT):
        tile = jnp.log(jnp.full((8, 128), k_ref[m], F32))
        for d in range(dims):
            tile = jnp.where(row == d + 1, sensitivity[m, d], tile)
        tile = jnp.where(row == 7, -decay[m], tile) * np.float32(LOG2E)
        table[m, 0] = pltpu.roll(tile, 4, 0)
        table[m, 1] = tile
    for i in range(material.shape[0] // 2):
        a, b = material[2 * i], material[2 * i + 1]
        for f in range(2):
            field[i, f, 84:88] = jnp.where(low_half, table[a, f], table[b, f])[4:8]


def remote(src, dst, send, recv, device):
    return pltpu.make_async_remote_copy(
        src_ref=src, dst_ref=dst, send_sem=send, recv_sem=recv,
        device_id=device, device_id_type=pl.DeviceIdType.MESH,
    )


def greet(space_count, chaos_count, space, chaos):
    barrier = pltpu.get_barrier_semaphore()
    peers = [(chaos + k) % chaos_count for k in range(1, chaos_count)]
    for peer in peers:
        pl.semaphore_signal(
            barrier, inc=1, device_id={"chaos": peer}, device_id_type=pl.DeviceIdType.MESH
        )
    for offset in OFFSETS:
        pl.semaphore_signal(
            barrier, inc=1, device_id={"space": (space + offset + space_count) % space_count},
            device_id_type=pl.DeviceIdType.MESH,
        )
    return barrier, peers


def evaluate(m, h, index, basis, store):
    row = lax.broadcasted_iota(jnp.int32, (8, 128), 0)
    aux = jnp.where(row < 4, pltpu.roll(m[80:88], 4, 0), h[80:88])
    damp = aux[7:8]
    arg = m * damp
    first = arg[0:8] + jnp.where(row < 7, aux, 0.0)
    rate = jnp.transpose(jnp.broadcast_to(damp * np.float32(LN2), (128, 128)))
    sides = [
        jnp.transpose(stacked(x, y, False))
        for x, y in (
            (m[0:80], m[80:88]), (h[0:80], h[80:88]),
            (jnp.concatenate([first, arg[8:80]], 0), arg[80:88]),
        )
    ]
    rows = [s[16 * c : 16 * c + 16] for c in range(8) for s in sides]
    r = jnp.dot(jnp.concatenate(rows, 0), basis, preferred_element_type=F32)
    for c in range(8):
        t = r[48 * c : 48 * c + 16]
        dt = r[48 * c + 16 : 48 * c + 32]
        k = jnp.exp2(r[48 * c + 32 : 48 * c + 48])
        speed = rate[16 * c : 16 * c + 16]
        dk = k * (dt * jnp.concatenate([speed] * (dt.shape[1] // 128), 1))
        block = 2 * index + c // 4
        at = slice(16 * (c % 4), 16 * (c % 4) + 16)
        store[block, 0, at] = t
        store[block, 1, at] = dt
        store[block, 2, at] = k
        store[block, 3, at] = dk


def columns(block, index, store, acc):
    width = 128
    shape = (SITES, width)
    row = lax.broadcasted_iota(jnp.int32, shape, 0)
    top = row == SITES - 1
    bottom = row == 0
    for part in range(store.shape[3] // width):
        at = slice(part * width, part * width + width)
        t, dt, k, dk = [store[block, f, :, at] for f in range(4)]
        up = [pltpu.roll(x, SITES - 1, 0) for x in (t, dt, k, dk)]
        gap = jnp.where(top, 0.0, t - up[0])
        step = jnp.where(top, 0.0, dt - up[1])
        both = k + up[2]
        change = dk + up[3]
        flow = both * gap
        turn = change * gap + both * step
        below = jnp.where(bottom, -4.0 * k * t, pltpu.roll(flow, 1, 0))
        under = jnp.where(bottom, -4.0 * (k * dt + dk * t), pltpu.roll(turn, 1, 0))
        acc[index, 0, :, at] = 2.0 * (flow - below)
        acc[index, 1, :, at] = 2.0 * (turn - under)


def pack_halo(e0, e1, field, out):
    low_half = lax.broadcasted_iota(jnp.int32, (1, 128), 1) < 64
    for f in range(2):
        x0 = half_turn(field[e0 // 2, f], e0 % 2 == 1)
        x1 = half_turn(field[e1 // 2, f], e1 % 2 == 0)
        out[f] = jnp.where(low_half, x0, x1)


def send_halo(space_count, space, picks, field, out, inbox, send, recv):
    copies = []
    for i, offset in enumerate(OFFSETS):
        target = (space + offset + space_count) % space_count
        pack_halo(picks[0, target], picks[1, target], field, out.at[i])
        copy = remote(out.at[i], inbox.at[i], send.at[i], recv.at[i], {"space": target})
        copy.start()
        copies.append(copy)
    return copies


def slot(neighbors, own, block, face, ranks, halo_depth):
    space, space_count, blocks = ranks
    entry = neighbors[face, block]
    away = jnp.maximum(entry - blocks, 0)
    distance = (space - away // halo_depth + space_count) % space_count
    order = jnp.where(
        distance == 1, 0, jnp.where(distance == space_count - 1, 1, jnp.where(distance == 2, 2, 3))
    )
    index = jnp.where(
        entry >= blocks, blocks + order * halo_depth + away % halo_depth, entry
    )
    return jnp.where(entry >= 0, index, own)


def faces(pair, local, ranks, halo_depth, neighbors, store, acc, bal):
    for j in range(2):
        own = 2 * pair + j
        mine = 2 * local + j
        others = [slot(neighbors, own, own, f, ranks, halo_depth) for f in range(4)]
        for c in range(SITES // 16):
            rows = slice(16 * c, 16 * c + 16)
            for part in range(store.shape[3] // 128):
                at = slice(part * 128, part * 128 + 128)
                t, dt, k, dk = [store[own, f, rows, at] for f in range(4)]
                flow = acc[mine, 0, rows, at]
                turn = acc[mine, 1, rows, at]
                for e in others:
                    gap = t - store[e, 0, rows, at]
                    step = dt - store[e, 1, rows, at]
                    both = k + store[e, 2, rows, at]
                    change = dk + store[e, 3, rows, at]
                    flow += both * gap
                    turn += change * gap + both * step
                for side, x in ((0, flow), (1, turn)):
                    high = x.astype(BF)
                    spot = slice(128 * side + 64 * j + 16 * c, 128 * side + 64 * j + 16 * c + 16)
                    bal[0, spot, at] = high
                    bal[1, spot, at] = (x - high.astype(F32)).astype(BF)


def project(nodes_at, right, bal):
    turned = (((1,), (1,)), ((), ()))
    one = lax.dot_general(right[:, nodes_at], bal[0], turned, preferred_element_type=F32)
    two = lax.dot_general(right[0:88, nodes_at], bal[1], turned, preferred_element_type=F32)
    return one[0:88] + one[88:176] + two


def keep(total, pair, first, mass, source, res, jvp):
    cols = pl.ds(pl.multiple_of(pair * 128, 128), 128)
    if first:
        res[:, cols] = (total[:, 0:128] - mass[...] * source[:, cols])[0:TERMS]
        jvp[:, cols] = total[0:TERMS, 128:256]
    else:
        res[:, cols] += total[0:TERMS, 0:128]
        jvp[:, cols] += total[0:TERMS, 128:256]


def whole_kernel(
    sizes, picks, k_ref, sensitivity, decay, material, neighbors, modes_far, heading_far,
    nodes_far, weights_far, codes_far, source, res, jvp,
    field, left, right, mass, store, acc, bal,
    nodes_t, weights, codes, table, out, inbox,
    send, recv, halo_send, halo_recv, near, local,
):
    space_count, chaos_count, pairs, halo_depth = sizes
    space = lax.axis_index("space")
    chaos = lax.axis_index("chaos")
    blocks = material.shape[0]
    base = chaos * pairs
    ranks = (space, space_count, blocks)
    barrier, peers = greet(space_count, chaos_count, space, chaos)
    loads = [
        pltpu.make_async_copy(
            far.at[:, i * 128 : i * 128 + 128], field.at[base + i, f, 0:TERMS],
            local.at[2 * i + f],
        )
        for i in range(pairs)
        for f, far in enumerate((modes_far, heading_far))
    ]
    extras = [
        pltpu.make_async_copy(a, b, near.at[i])
        for i, (a, b) in enumerate(
            [(nodes_far, nodes_t), (weights_far, weights), (codes_far, codes)]
        )
    ]
    for load in loads + extras:
        load.start()
    for load in loads:
        load.wait()
    pl.semaphore_wait(barrier, len(peers) + len(OFFSETS))

    def block(owner, first, count):
        return field.at[pl.ds(owner * pairs + first, count), :, 0:TERMS]

    def passing(i, owner, first, count, target):
        ref = block(owner, first, count)
        return remote(ref, ref, send.at[i], recv.at[i], {"chaos": target})

    width = store.shape[3]

    def evaluate_span(start, count, nodes_at=slice(0, width)):
        def body(i, carry):
            evaluate(
                field[start + i, 0], field[start + i, 1], start + i, left[:, nodes_at], store
            )
            return carry

        lax.fori_loop(0, count, body, 0)

    def own_columns():
        def body(i, carry):
            columns(2 * base + i, i, store, acc)
            return carry

        lax.fori_loop(0, 2 * pairs, body, 0)

    def finish(nodes_at, first):
        def late(pair, carry):
            faces(base + pair, pair, ranks, halo_depth, neighbors, store, acc, bal)
            keep(project(nodes_at, right, bal), pair, first, mass, source, res, jvp)
            return carry

        lax.fori_loop(0, pairs, late, 0)

    def mine():
        fill_aux(k_ref, sensitivity, decay, material, table, field)
        for load in extras:
            load.wait()
        fill_tables(nodes_t, weights, codes, left, right, mass)
        evaluate_span(base, pairs)
        own_columns()

    copies = [passing(i, chaos, 0, pairs, t) for i, t in enumerate(peers)]
    for copy in copies:
        copy.start()
    mine()
    for i, copy in enumerate(copies):
        copy.wait_recv()
    halo = send_halo(space_count, space, picks, field, out, inbox, halo_send, halo_recv)
    for i in range(1, chaos_count):
        evaluate_span(((chaos + i) % chaos_count) * pairs, pairs)
    for i, copy in enumerate(halo):
        copy.wait_recv()
        evaluate(inbox[i, 0], inbox[i, 1], blocks // 2 + i, left[:, 0:width], store)
    finish(slice(0, width), True)

    def again(part, carry):
        nodes_at = pl.ds(pl.multiple_of(part * width, width), width)
        evaluate_span(0, blocks // 2, nodes_at)
        for i in range(len(OFFSETS)):
            evaluate(inbox[i, 0], inbox[i, 1], blocks // 2 + i, left[:, nodes_at], store)
        own_columns()
        finish(nodes_at, False)
        return carry

    if left.shape[1] > width:
        lax.fori_loop(1, left.shape[1] // width, again, 0)
    for copy in copies + halo:
        copy.wait_send()


def per_device(
    chaos_modes, newton_heading, source, nodes, weights, k_ref, sensitivity, decay,
    material, neighbors, send_list,
):
    space_count = lax.axis_size("space")
    cells = chaos_modes.shape[1]
    pairs = cells // 128
    halo_depth = send_list.shape[2]
    queue = nodes.shape[0]
    span = min(queue, SPAN)
    blocks = material.shape[0]
    far = pl.BlockSpec(memory_space=pltpu.HBM)
    vmem = pl.BlockSpec(memory_space=pltpu.VMEM)
    smem = pl.BlockSpec(memory_space=pltpu.SMEM)
    return pl.pallas_call(
        functools.partial(
            whole_kernel, (space_count, lax.axis_size("chaos"), pairs, halo_depth)
        ),
        out_shape=[jax.ShapeDtypeStruct((TERMS, cells), F32)] * 2,
        in_specs=[smem] * 6 + [far] * 5 + [vmem],
        out_specs=[vmem] * 2,
        scratch_shapes=[
            pltpu.VMEM((blocks // 2, 2, 88, 128), F32),
            pltpu.VMEM((256, queue), BF),
            pltpu.VMEM((176, queue), BF),
            pltpu.VMEM((88, 1), F32),
            pltpu.VMEM((blocks + 8, 4, SITES, span), F32),
            pltpu.VMEM((2 * pairs, 2, SITES, span), F32),
            pltpu.VMEM((2, 256, span), BF),
            pltpu.VMEM((nodes.shape[1], queue), F32),
            pltpu.VMEM((1, queue), F32),
            pltpu.VMEM((8, 128), F32),
            pltpu.VMEM((NMAT, 2, 8, 128), F32),
            pltpu.VMEM((4, 2, 88, 128), F32),
            pltpu.VMEM((4, 2, 88, 128), F32),
            pltpu.SemaphoreType.DMA((16,)),
            pltpu.SemaphoreType.DMA((16,)),
            pltpu.SemaphoreType.DMA((4,)),
            pltpu.SemaphoreType.DMA((4,)),
            pltpu.SemaphoreType.DMA((3,)),
            pltpu.SemaphoreType.DMA((2 * pairs,)),
        ],
        compiler_params=pltpu.CompilerParams(
            collective_id=0, has_side_effects=True, vmem_limit_bytes=60 * 1024 * 1024
        ),
    )(
        send_list[0].T, k_ref, sensitivity, decay, material, neighbors.T, chaos_modes,
        newton_heading, nodes.T, weights[None, :], jnp.asarray(order_codes(nodes.shape[1])),
        source[None, :],
    )


def paired_kernel(
    sizes, k_ref, sensitivity, decay, material_far, neighbors_far, picks_far, modes_far,
    heading_far, nodes_far, weights_far, codes_far, source_far, total,
    field, mine, left, right, mass, store, acc, bal, stage, source,
    nodes_t, weights, codes, table, out, inbox, material, neighbors, picks,
    local, near, first_send, first_recv, on_send, send, recv, halo_send, halo_recv,
    back_send, back_recv,
):
    space_count, pairs, halo_depth = sizes
    space = lax.axis_index("space")
    chaos = lax.axis_index("chaos")
    z, core = space // 2, space % 2
    y, x = chaos // 2, chaos % 2
    home = core == x
    part = 2 * z + x
    half, piece = pairs // 2, pairs // 4
    blocks = material.shape[0]
    ranks = (part, space_count, blocks)
    rank_x, rank_y, rank_d = 2 * y + 1 - x, 2 - 2 * y + x, 3 - chaos

    def device(index, rank):
        return {"space": index, "chaos": rank}

    sibling = device(2 * z + 1 - core, chaos)

    def offset(j):
        return (part + (1 + core) * (1 - 2 * j) + space_count) % space_count

    facing = [device(2 * (offset(j) // 2) + core, 2 * y + offset(j) % 2) for j in range(2)]
    barrier = pltpu.get_barrier_semaphore()
    peers = [sibling] + [device(2 * z + k, r) for k in range(2) for r in (rank_x, rank_y)]
    for peer in peers + facing:
        pl.semaphore_signal(
            barrier, inc=1, device_id=peer, device_id_type=pl.DeviceIdType.MESH
        )
    loads = [
        pltpu.make_async_copy(
            far.at[:, i * 128 : i * 128 + 128], mine.at[i, f], local.at[2 * i + f]
        )
        for i in range(pairs)
        for f, far in enumerate((modes_far, heading_far))
    ]
    extras = [
        pltpu.make_async_copy(a, b, near.at[i])
        for i, (a, b) in enumerate(
            [(nodes_far, nodes_t), (weights_far, weights), (codes_far, codes)]
        )
    ]
    for load in loads + extras:
        load.start()
    for load in loads:
        load.wait()
    pl.semaphore_wait(barrier, len(peers + facing))

    def span(rank, first, count):
        return field.at[pl.ds(rank * pairs + first, count), :, 0:TERMS]

    firsts = []
    kind = jnp.where(home, 2, 0)
    rank_to = jnp.where(home, rank_y, rank_x)
    for p in range(2):
        for k in range(2):
            at = k * half + p * piece
            i = 2 * p + k
            firsts.append(
                remote(
                    mine.at[at : at + piece], span(chaos, at, piece), first_send.at[i],
                    recv.at[kind + p], device(2 * z + k, rank_to),
                )
            )
    width = half * 128
    heat = [source_far.at[:, k * width : k * width + width] for k in range(2)]
    crossing = [
        remote(
            heat[k], source.at[0], first_send.at[4 + k], first_recv.at[5],
            device(2 * z + k, rank_x),
        )
        for k in range(2)
    ]

    def heat_of(k):
        return source_far.at[:, pl.ds(pl.multiple_of(k * width, 128), width)]

    tables = ((material_far, material), (neighbors_far, neighbors), (picks_far, picks))
    given = [
        remote(a, b, on_send.at[i], first_recv.at[i], sibling)
        for i, (a, b) in enumerate(tables)
    ] + [
        remote(mine, span(chaos, 0, pairs), on_send.at[3], first_recv.at[3], sibling),
        remote(heat_of(1 - core), source.at[1], on_send.at[4], first_recv.at[4], sibling),
    ]
    taken = [
        pltpu.make_async_copy(a, b, on_send.at[5 + i]) for i, (a, b) in enumerate(tables)
    ] + [
        pltpu.make_async_copy(mine, span(chaos, 0, pairs), on_send.at[8]),
        pltpu.make_async_copy(heat_of(core), source.at[1], on_send.at[9]),
    ]

    for copy in firsts:
        copy.start()

    @pl.when(home)
    def _():
        for copy in given + taken:
            copy.start()

    @pl.when(jnp.logical_not(home))
    def _():
        for copy in crossing:
            copy.start()

    for load in extras:
        load.wait()
    fill_tables(nodes_t, weights, codes, left, right, mass)

    @pl.when(home)
    def _():
        for copy in taken:
            copy.wait()

    @pl.when(jnp.logical_not(home))
    def _():
        for copy in given:
            copy.wait_recv()

    fill_aux(k_ref, sensitivity, decay, material, table, field)

    def evaluate_span(start, count):
        def body(i, carry):
            evaluate(field[start + i, 0], field[start + i, 1], start + i, left[...], store)
            return carry

        lax.fori_loop(0, count, body, 0)

    def own_columns(rank, at):
        def body(i, carry):
            columns(2 * (rank * pairs + core * half) + i, 2 * at + i, store, acc)
            return carry

        lax.fori_loop(0, 2 * half, body, 0)

    def region(kind, p, side):
        rank = (rank_x, rank_y, rank_d)[kind]
        return rank, jnp.where(side == 0, core, 1 - core) * half + p * piece

    later = []

    def arrived(kind, p, side):
        ref = span(*region(kind, p, side), piece)
        remote(ref, ref, send.at[0], recv.at[6 * side + 2 * kind + p], sibling).wait_recv()
        return ref

    def hand_on(ref, kind, p, side, target):
        copy = remote(
            ref, ref, send.at[len(later)], recv.at[6 * side + 2 * kind + p], target
        )
        copy.start()
        later.append(copy)

    def take(kind, p):
        ref = arrived(kind, p, 0)
        if kind == 0:
            hand_on(ref, 2, p, 0, device(space, rank_y))
        hand_on(ref, kind, p, 1, sibling)

    def work(kind, p):
        for side in range(2):
            if side == 1:
                arrived(kind, p, 1)
            rank, first = region(kind, p, side)
            evaluate_span(rank * pairs + first, piece)

    evaluate_span(chaos * pairs, pairs)
    take(0, 0)
    take(1, 0)
    work(0, 0)
    own_columns(chaos, half)
    take(0, 1)
    take(1, 1)
    work(1, 0)
    work(0, 1)
    own_columns(rank_x, 0)
    work(1, 1)
    take(2, 0)
    work(2, 0)
    take(2, 1)
    arrived(2, 1, 1)
    halo = []
    for j in range(2):
        pack_halo(picks[0, offset(j)], picks[1, offset(j)], field, out.at[j])
        copy = remote(
            out.at[j], inbox.at[2 * core + j], halo_send.at[j], halo_recv.at[j], facing[j]
        )
        copy.start()
        halo.append(copy)
    for side in range(2):
        rank, first = region(2, 1, side)
        evaluate_span(rank * pairs + first, piece)

    def halo_pair(i):
        evaluate(inbox[i, 0], inbox[i, 1], blocks // 2 + i, left[...], store)

    for j in range(2):
        halo[j].wait_recv()
        ref = inbox.at[2 * core + j]
        copy = remote(ref, ref, halo_send.at[2 + j], halo_recv.at[2 + j], sibling)
        copy.start()
        later.append(copy)
    for j in range(2):
        halo_pair(2 * core + j)
    for j in range(2):
        ref = inbox.at[2 - 2 * core + j]
        remote(ref, ref, halo_send.at[2 + j], halo_recv.at[2 + j], sibling).wait_recv()
        halo_pair(2 - 2 * core + j)

    def result(i):
        return stage.at[i, :, 0:TERMS]

    def place(side, i):
        at = pl.multiple_of((side * half + i) * 128, 128)
        return total.at[:, :, pl.ds(at, 128)]

    def late(rank, at, i):
        faces(rank * pairs + core * half + i, at + i, ranks, halo_depth, neighbors, store, acc, bal)
        sums = project(slice(0, store.shape[3]), right, bal)
        warm = source[at // half, :, pl.ds(pl.multiple_of(i * 128, 128), 128)]
        stage[at + i, 0] = sums[:, 0:128] - mass[...] * warm
        stage[at + i, 1] = sums[:, 128:256]

    def back_across(i):
        return remote(
            result(i), place(core, i), back_send.at[i], back_recv.at[core * half + i],
            device(part, rank_x),
        )

    def back_beside(i):
        return remote(
            result(half + i), place(core, i), back_send.at[half + i],
            back_recv.at[2 * half + i], sibling,
        )

    def back_here(i):
        return pltpu.make_async_copy(
            result(half + i), place(core, i), back_send.at[half + i]
        )

    def far_pair(i, carry):
        late(rank_x, 0, i)
        back_across(i).start()
        return carry

    def near_pair(i, carry):
        late(chaos, half, i)

        @pl.when(home)
        def _():
            back_here(i).start()

        @pl.when(jnp.logical_not(home))
        def _():
            back_beside(i).start()

        return carry

    remote(heat[0], source.at[0], first_send.at[0], first_recv.at[5], sibling).wait_recv()
    lax.fori_loop(0, half, far_pair, 0)
    lax.fori_loop(0, half, near_pair, 0)
    for copy in firsts + later + halo:
        copy.wait_send()
    for i in range(half):
        back_across(i).wait_send()

    @pl.when(home)
    def _():
        for copy in given:
            copy.wait_send()
        for i in range(half):
            back_here(i).wait()
            remote(
                result(half + i), place(1 - core, i), back_send.at[half + i],
                back_recv.at[2 * half + i], sibling,
            ).wait_recv()

    @pl.when(jnp.logical_not(home))
    def _():
        for copy in crossing:
            copy.wait_send()
        for i in range(half):
            back_beside(i).wait_send()
            for k in range(2):
                remote(
                    result(i), place(k, i), back_send.at[i], back_recv.at[k * half + i],
                    sibling,
                ).wait_recv()


def part_kernel(total, res, jvp, held, into, onto):
    half = total.shape[2] // 2
    cuts = [(i, k * half) for i in range(2) for k in range(2)]
    reads, writes = [], []
    for j, (i, at) in enumerate(cuts):
        there = (res, jvp)[i].at[:, at : at + half]
        reads.append(pltpu.make_async_copy(total.at[i, :, at : at + half], held.at[j], into.at[j]))
        writes.append(pltpu.make_async_copy(held.at[j], there, onto.at[j]))
    for copy in reads:
        copy.start()
    for read, write in zip(reads, writes):
        read.wait()
        write.start()
    for copy in writes:
        copy.wait()


def parted(total):
    rows, cells = total.shape[1:]
    far = pl.BlockSpec(memory_space=pltpu.HBM)
    return tuple(
        pl.pallas_call(
            part_kernel,
            out_shape=[jax.ShapeDtypeStruct((rows, cells), F32)] * 2,
            in_specs=[far],
            out_specs=[far] * 2,
            scratch_shapes=[
                pltpu.VMEM((4, rows, cells // 2), F32),
                pltpu.SemaphoreType.DMA((4,)), pltpu.SemaphoreType.DMA((4,)),
            ],
        )(total)
    )


def paired_device(
    chaos_modes, newton_heading, source, nodes, weights, k_ref, sensitivity, decay,
    material, neighbors, send_list,
):
    space_count = lax.axis_size("space")
    cells = chaos_modes.shape[1]
    pairs = cells // 128
    half = pairs // 2
    halo_depth = send_list.shape[2]
    queue = nodes.shape[0]
    blocks = material.shape[0]
    far = pl.BlockSpec(memory_space=pltpu.HBM)
    smem = pl.BlockSpec(memory_space=pltpu.SMEM)
    dma = pltpu.SemaphoreType.DMA
    total = pl.pallas_call(
        functools.partial(paired_kernel, (space_count, pairs, halo_depth)),
        out_shape=jax.ShapeDtypeStruct((2, TERMS, cells), F32),
        in_specs=[smem] * 3 + [far] * 9,
        out_specs=far,
        scratch_shapes=[
            pltpu.VMEM((blocks // 2, 2, 88, 128), F32),
            pltpu.VMEM((pairs, 2, TERMS, 128), F32),
            pltpu.VMEM((256, queue), BF),
            pltpu.VMEM((176, queue), BF),
            pltpu.VMEM((88, 1), F32),
            pltpu.VMEM((blocks + 8, 4, SITES, queue), F32),
            pltpu.VMEM((2 * pairs, 2, SITES, queue), F32),
            pltpu.VMEM((2, 256, queue), BF),
            pltpu.VMEM((pairs, 2, 88, 128), F32),
            pltpu.VMEM((2, 1, half * 128), F32),
            pltpu.VMEM((nodes.shape[1], queue), F32),
            pltpu.VMEM((1, queue), F32),
            pltpu.VMEM((8, 128), F32),
            pltpu.VMEM((NMAT, 2, 8, 128), F32),
            pltpu.VMEM((2, 2, 88, 128), F32),
            pltpu.VMEM((4, 2, 88, 128), F32),
            pltpu.SMEM((blocks,), jnp.int32),
            pltpu.SMEM((4, blocks), jnp.int32),
            pltpu.SMEM((halo_depth, space_count), jnp.int32),
            dma((2 * pairs,)), dma((3,)), dma((6,)), dma((6,)), dma((10,)), dma((8,)),
            dma((12,)), dma((4,)), dma((4,)), dma((2 * half,)), dma((3 * half,)),
        ],
        compiler_params=pltpu.CompilerParams(
            collective_id=1, has_side_effects=True, vmem_limit_bytes=60 * 1024 * 1024
        ),
    )(
        k_ref, sensitivity, decay, material, neighbors.T, send_list[0].T, chaos_modes,
        newton_heading, nodes.T, weights[None, :], jnp.asarray(order_codes(nodes.shape[1])),
        source[None, :],
    )
    return parted(total)


def device_program(*args):
    modes, nodes, halo_depth = args[0], args[3], args[10].shape[2]
    space_count = lax.axis_size("space")
    paired = lax.axis_size("chaos") == 4 and space_count % 2 == 0 and space_count > 4
    fits = modes.shape[1] % 512 == 0 and nodes.shape[0] <= SPAN and halo_depth == 2
    return (paired_device if paired and fits else per_device)(*args)


def solution(mesh):
    return jax.shard_map(
        device_program,
        mesh=mesh,
        in_specs=(
            P(None, ("space", "chaos")),
            P(None, ("space", "chaos")),
            P(("space", "chaos")),
            P(), P(), P(), P(), P(),
            P("space"),
            P("space", None),
            P("space", None, None),
        ),
        out_specs=(P(None, ("space", "chaos")), P(None, ("space", "chaos"))),
        check_vma=False,
    )
```

```python
import functools
import math

import jax
import jax.numpy as jnp
import numpy as np
from jax import lax
from jax.experimental import pallas as pl
from jax.experimental.pallas import tpu as pltpu
from jax.sharding import PartitionSpec as P

NMAT = 4
SITES = 64
TERMS = 84
MAIN = 80
LOG2E = 1.0 / math.log(2.0)
LN2 = math.log(2.0)
OFFSETS = (1, -1, 2, -2)
SPAN = 512
BF = jnp.bfloat16
F32 = jnp.float32


def compositions(remaining, places):
    if places == 1:
        return [[remaining]]
    listing = []
    for leading in range(remaining, -1, -1):
        for trailing in compositions(remaining - leading, places - 1):
            listing.append([leading] + trailing)
    return listing


def chaos_orders(variables):
    listing = []
    for degree in range(4):
        listing = listing + compositions(degree, variables)
    return np.array(listing, dtype=np.int32)


def half_turn(x, wanted):
    return jnp.where(wanted, pltpu.roll(x, 64, 1), x)


def factors(x, o):
    second = (x * x - 1.0) * np.float32(1.0 / math.sqrt(2.0))
    third = (x * x * x - 3.0 * x) * np.float32(1.0 / math.sqrt(6.0))
    return jnp.where(o == 0, 1.0, jnp.where(o == 1, x, jnp.where(o == 2, second, third)))


def order_codes(dims):
    orders = chaos_orders(dims)
    code = (orders * 4 ** np.arange(dims)[None, :]).sum(1)
    out = np.zeros((8, 128), np.float32)
    out[0, :TERMS] = code
    return out


def upright(row):
    return jnp.transpose(jnp.broadcast_to(row, (128, 128)))


def stacked(main, tail, lower):
    row = lax.broadcasted_iota(jnp.int32, tail.shape, 0)
    high = main.astype(BF)
    low = (main - high.astype(F32)).astype(BF)
    tail_high = tail.astype(BF).astype(F32)
    tail_low = tail - tail_high
    if lower:
        parts = [high, high, low]
        ends = [jnp.where(row < 4, tail_high, pltpu.roll(tail_high, 4, 0)), tail_low]
    else:
        parts = [high, low, high]
        ends = [jnp.where(row < 4, tail_high, pltpu.roll(tail_low, 4, 0)), tail_high]
    ends[1] = jnp.where(row < 4, ends[1], 0.0)
    return jnp.concatenate(parts + [jnp.concatenate(ends, 0).astype(BF)], 0)


def fill_tables(nodes_t, weights, codes, left, right, mass):
    dims = nodes_t.shape[0]
    code = upright(codes[0:1, 0:128])[0:88].astype(jnp.int32)
    row = lax.broadcasted_iota(jnp.int32, (88, 1), 0)
    mass[...] = jnp.zeros(mass.shape, F32)

    def body(part, carry):
        span = pl.ds(pl.multiple_of(part * 128, 128), 128)
        value = jnp.ones((88, 128), F32)
        for d in range(dims):
            value = value * factors(nodes_t[d : d + 1, span], (code // 4**d) % 4)
        value = jnp.where(row < TERMS, value, 0.0)
        left[:, span] = stacked(value[0:80], value[80:88], True)
        value = value * weights[:, span]
        mass[...] += jnp.sum(value, axis=1, keepdims=True)
        value = value * 0.25
        high = value.astype(BF).astype(F32)
        right[:, span] = jnp.concatenate([high, value - high], 0).astype(BF)
        return carry

    lax.fori_loop(0, nodes_t.shape[1] // 128, body, 0)


def fill_aux(k_ref, sensitivity, decay, material, table, field):
    row = lax.broadcasted_iota(jnp.int32, (8, 128), 0)
    low_half = lax.broadcasted_iota(jnp.int32, (8, 128), 1) < 64
    dims = sensitivity.shape[1]
    for m in range(NMAT):
        tile = jnp.log(jnp.full((8, 128), k_ref[m], F32))
        for d in range(dims):
            tile = jnp.where(row == d + 1, sensitivity[m, d], tile)
        tile = jnp.where(row == 7, -decay[m], tile) * np.float32(LOG2E)
        table[m, 0] = pltpu.roll(tile, 4, 0)
        table[m, 1] = tile
    for i in range(material.shape[0] // 2):
        a, b = material[2 * i], material[2 * i + 1]
        for f in range(2):
            field[i, f, 84:88] = jnp.where(low_half, table[a, f], table[b, f])[4:8]


def remote(src, dst, send, recv, device):
    return pltpu.make_async_remote_copy(
        src_ref=src, dst_ref=dst, send_sem=send, recv_sem=recv,
        device_id=device, device_id_type=pl.DeviceIdType.MESH,
    )


def greet(space_count, chaos_count, space, chaos):
    barrier = pltpu.get_barrier_semaphore()
    peers = [(chaos + k) % chaos_count for k in range(1, chaos_count)]
    for peer in peers:
        pl.semaphore_signal(
            barrier, inc=1, device_id={"chaos": peer}, device_id_type=pl.DeviceIdType.MESH
        )
    for offset in OFFSETS:
        pl.semaphore_signal(
            barrier, inc=1, device_id={"space": (space + offset + space_count) % space_count},
            device_id_type=pl.DeviceIdType.MESH,
        )
    return barrier, peers


def evaluate(m, h, index, basis, store):
    row = lax.broadcasted_iota(jnp.int32, (8, 128), 0)
    aux = jnp.where(row < 4, pltpu.roll(m[80:88], 4, 0), h[80:88])
    damp = aux[7:8]
    arg = m * damp
    first = arg[0:8] + jnp.where(row < 7, aux, 0.0)
    rate = jnp.transpose(jnp.broadcast_to(damp * np.float32(LN2), (128, 128)))
    sides = [
        jnp.transpose(stacked(x, y, False))
        for x, y in (
            (m[0:80], m[80:88]), (h[0:80], h[80:88]),
            (jnp.concatenate([first, arg[8:80]], 0), arg[80:88]),
        )
    ]
    rows = [s[16 * c : 16 * c + 16] for c in range(8) for s in sides]
    r = jnp.dot(jnp.concatenate(rows, 0), basis, preferred_element_type=F32)
    for c in range(8):
        t = r[48 * c : 48 * c + 16]
        dt = r[48 * c + 16 : 48 * c + 32]
        k = jnp.exp2(r[48 * c + 32 : 48 * c + 48])
        speed = rate[16 * c : 16 * c + 16]
        dk = k * (dt * jnp.concatenate([speed] * (dt.shape[1] // 128), 1))
        block = 2 * index + c // 4
        at = slice(16 * (c % 4), 16 * (c % 4) + 16)
        store[block, 0, at] = t
        store[block, 1, at] = dt
        store[block, 2, at] = k
        store[block, 3, at] = dk


def columns(block, index, store, acc):
    width = 128
    shape = (SITES, width)
    row = lax.broadcasted_iota(jnp.int32, shape, 0)
    top = row == SITES - 1
    bottom = row == 0
    for part in range(store.shape[3] // width):
        at = slice(part * width, part * width + width)
        t, dt, k, dk = [store[block, f, :, at] for f in range(4)]
        up = [pltpu.roll(x, SITES - 1, 0) for x in (t, dt, k, dk)]
        gap = jnp.where(top, 0.0, t - up[0])
        step = jnp.where(top, 0.0, dt - up[1])
        both = k + up[2]
        change = dk + up[3]
        flow = both * gap
        turn = change * gap + both * step
        below = jnp.where(bottom, -4.0 * k * t, pltpu.roll(flow, 1, 0))
        under = jnp.where(bottom, -4.0 * (k * dt + dk * t), pltpu.roll(turn, 1, 0))
        acc[index, 0, :, at] = 2.0 * (flow - below)
        acc[index, 1, :, at] = 2.0 * (turn - under)


def pack_halo(e0, e1, field, out):
    low_half = lax.broadcasted_iota(jnp.int32, (1, 128), 1) < 64
    for f in range(2):
        x0 = half_turn(field[e0 // 2, f], e0 % 2 == 1)
        x1 = half_turn(field[e1 // 2, f], e1 % 2 == 0)
        out[f] = jnp.where(low_half, x0, x1)


def send_halo(space_count, space, picks, field, out, inbox, send, recv):
    copies = []
    for i, offset in enumerate(OFFSETS):
        target = (space + offset + space_count) % space_count
        pack_halo(picks[0, target], picks[1, target], field, out.at[i])
        copy = remote(out.at[i], inbox.at[i], send.at[i], recv.at[i], {"space": target})
        copy.start()
        copies.append(copy)
    return copies


def slot(neighbors, own, block, face, ranks, halo_depth):
    space, space_count, blocks = ranks
    entry = neighbors[face, block]
    away = jnp.maximum(entry - blocks, 0)
    distance = (space - away // halo_depth + space_count) % space_count
    order = jnp.where(
        distance == 1, 0, jnp.where(distance == space_count - 1, 1, jnp.where(distance == 2, 2, 3))
    )
    index = jnp.where(
        entry >= blocks, blocks + order * halo_depth + away % halo_depth, entry
    )
    return jnp.where(entry >= 0, index, own)


def faces(pair, local, ranks, halo_depth, neighbors, store, acc, bal):
    for j in range(2):
        own = 2 * pair + j
        mine = 2 * local + j
        others = [slot(neighbors, own, own, f, ranks, halo_depth) for f in range(4)]
        for c in range(SITES // 16):
            rows = slice(16 * c, 16 * c + 16)
            for part in range(store.shape[3] // 128):
                at = slice(part * 128, part * 128 + 128)
                t, dt, k, dk = [store[own, f, rows, at] for f in range(4)]
                flow = acc[mine, 0, rows, at]
                turn = acc[mine, 1, rows, at]
                for e in others:
                    gap = t - store[e, 0, rows, at]
                    step = dt - store[e, 1, rows, at]
                    both = k + store[e, 2, rows, at]
                    change = dk + store[e, 3, rows, at]
                    flow += both * gap
                    turn += change * gap + both * step
                for side, x in ((0, flow), (1, turn)):
                    high = x.astype(BF)
                    spot = slice(128 * side + 64 * j + 16 * c, 128 * side + 64 * j + 16 * c + 16)
                    bal[0, spot, at] = high
                    bal[1, spot, at] = (x - high.astype(F32)).astype(BF)


def project(nodes_at, right, bal):
    turned = (((1,), (1,)), ((), ()))
    one = lax.dot_general(right[:, nodes_at], bal[0], turned, preferred_element_type=F32)
    two = lax.dot_general(right[0:88, nodes_at], bal[1], turned, preferred_element_type=F32)
    return one[0:88] + one[88:176] + two


def keep(total, pair, first, mass, source, res, jvp):
    cols = pl.ds(pl.multiple_of(pair * 128, 128), 128)
    if first:
        res[:, cols] = (total[:, 0:128] - mass[...] * source[:, cols])[0:TERMS]
        jvp[:, cols] = total[0:TERMS, 128:256]
    else:
        res[:, cols] += total[0:TERMS, 0:128]
        jvp[:, cols] += total[0:TERMS, 128:256]


def whole_kernel(
    sizes, picks, k_ref, sensitivity, decay, material, neighbors, modes_far, heading_far,
    nodes_far, weights_far, codes_far, source, res, jvp,
    field, left, right, mass, store, acc, bal,
    nodes_t, weights, codes, table, out, inbox,
    send, recv, halo_send, halo_recv, near, local,
):
    space_count, chaos_count, pairs, halo_depth = sizes
    space = lax.axis_index("space")
    chaos = lax.axis_index("chaos")
    blocks = material.shape[0]
    base = chaos * pairs
    ranks = (space, space_count, blocks)
    barrier, peers = greet(space_count, chaos_count, space, chaos)
    loads = [
        pltpu.make_async_copy(
            far.at[:, i * 128 : i * 128 + 128], field.at[base + i, f, 0:TERMS],
            local.at[2 * i + f],
        )
        for i in range(pairs)
        for f, far in enumerate((modes_far, heading_far))
    ]
    extras = [
        pltpu.make_async_copy(a, b, near.at[i])
        for i, (a, b) in enumerate(
            [(nodes_far, nodes_t), (weights_far, weights), (codes_far, codes)]
        )
    ]
    for load in loads + extras:
        load.start()
    for load in loads:
        load.wait()
    pl.semaphore_wait(barrier, len(peers) + len(OFFSETS))

    def block(owner, first, count):
        return field.at[pl.ds(owner * pairs + first, count), :, 0:TERMS]

    def passing(i, owner, first, count, target):
        ref = block(owner, first, count)
        return remote(ref, ref, send.at[i], recv.at[i], {"chaos": target})

    width = store.shape[3]

    def evaluate_span(start, count, nodes_at=slice(0, width)):
        def body(i, carry):
            evaluate(
                field[start + i, 0], field[start + i, 1], start + i, left[:, nodes_at], store
            )
            return carry

        lax.fori_loop(0, count, body, 0)

    def own_columns():
        def body(i, carry):
            columns(2 * base + i, i, store, acc)
            return carry

        lax.fori_loop(0, 2 * pairs, body, 0)

    def finish(nodes_at, first):
        def late(pair, carry):
            faces(base + pair, pair, ranks, halo_depth, neighbors, store, acc, bal)
            keep(project(nodes_at, right, bal), pair, first, mass, source, res, jvp)
            return carry

        lax.fori_loop(0, pairs, late, 0)

    def mine():
        fill_aux(k_ref, sensitivity, decay, material, table, field)
        for load in extras:
            load.wait()
        fill_tables(nodes_t, weights, codes, left, right, mass)
        evaluate_span(base, pairs)
        own_columns()

    copies = [passing(i, chaos, 0, pairs, t) for i, t in enumerate(peers)]
    for copy in copies:
        copy.start()
    mine()
    for i, copy in enumerate(copies):
        copy.wait_recv()
    halo = send_halo(space_count, space, picks, field, out, inbox, halo_send, halo_recv)
    for i in range(1, chaos_count):
        evaluate_span(((chaos + i) % chaos_count) * pairs, pairs)
    for i, copy in enumerate(halo):
        copy.wait_recv()
        evaluate(inbox[i, 0], inbox[i, 1], blocks // 2 + i, left[:, 0:width], store)
    finish(slice(0, width), True)

    def again(part, carry):
        nodes_at = pl.ds(pl.multiple_of(part * width, width), width)
        evaluate_span(0, blocks // 2, nodes_at)
        for i in range(len(OFFSETS)):
            evaluate(inbox[i, 0], inbox[i, 1], blocks // 2 + i, left[:, nodes_at], store)
        own_columns()
        finish(nodes_at, False)
        return carry

    if left.shape[1] > width:
        lax.fori_loop(1, left.shape[1] // width, again, 0)
    for copy in copies + halo:
        copy.wait_send()


def per_device(
    chaos_modes, newton_heading, source, nodes, weights, k_ref, sensitivity, decay,
    material, neighbors, send_list,
):
    space_count = lax.axis_size("space")
    cells = chaos_modes.shape[1]
    pairs = cells // 128
    halo_depth = send_list.shape[2]
    queue = nodes.shape[0]
    span = min(queue, SPAN)
    blocks = material.shape[0]
    far = pl.BlockSpec(memory_space=pltpu.HBM)
    vmem = pl.BlockSpec(memory_space=pltpu.VMEM)
    smem = pl.BlockSpec(memory_space=pltpu.SMEM)
    return pl.pallas_call(
        functools.partial(
            whole_kernel, (space_count, lax.axis_size("chaos"), pairs, halo_depth)
        ),
        out_shape=[jax.ShapeDtypeStruct((TERMS, cells), F32)] * 2,
        in_specs=[smem] * 6 + [far] * 5 + [vmem],
        out_specs=[vmem] * 2,
        scratch_shapes=[
            pltpu.VMEM((blocks // 2, 2, 88, 128), F32),
            pltpu.VMEM((256, queue), BF),
            pltpu.VMEM((176, queue), BF),
            pltpu.VMEM((88, 1), F32),
            pltpu.VMEM((blocks + 8, 4, SITES, span), F32),
            pltpu.VMEM((2 * pairs, 2, SITES, span), F32),
            pltpu.VMEM((2, 256, span), BF),
            pltpu.VMEM((nodes.shape[1], queue), F32),
            pltpu.VMEM((1, queue), F32),
            pltpu.VMEM((8, 128), F32),
            pltpu.VMEM((NMAT, 2, 8, 128), F32),
            pltpu.VMEM((4, 2, 88, 128), F32),
            pltpu.VMEM((4, 2, 88, 128), F32),
            pltpu.SemaphoreType.DMA((16,)),
            pltpu.SemaphoreType.DMA((16,)),
            pltpu.SemaphoreType.DMA((4,)),
            pltpu.SemaphoreType.DMA((4,)),
            pltpu.SemaphoreType.DMA((3,)),
            pltpu.SemaphoreType.DMA((2 * pairs,)),
        ],
        compiler_params=pltpu.CompilerParams(
            collective_id=0, has_side_effects=True, vmem_limit_bytes=60 * 1024 * 1024
        ),
    )(
        send_list[0].T, k_ref, sensitivity, decay, material, neighbors.T, chaos_modes,
        newton_heading, nodes.T, weights[None, :], jnp.asarray(order_codes(nodes.shape[1])),
        source[None, :],
    )


def paired_kernel(
    sizes, k_far, sensitivity_far, decay_far, material_far, neighbors_far, picks_far, modes_far,
    heading_far, nodes_far, weights_far, codes_far, source_far, total,
    field, mine, left, right, mass, store, acc, bal, stage, source,
    nodes_t, weights, codes, table, out, inbox, k_ref, sensitivity, decay, material,
    neighbors, picks,
    local, near, first_send, first_recv, on_send, send, recv, halo_send, halo_recv,
    back_send, back_recv,
):
    space_count, pairs, halo_depth = sizes
    space = lax.axis_index("space")
    chaos = lax.axis_index("chaos")
    z, core = space // 2, space % 2
    y, x = chaos // 2, chaos % 2
    home = core == x
    part = 2 * z + x
    half, piece = pairs // 2, pairs // 4
    blocks = material.shape[0]
    ranks = (part, space_count, blocks)
    rank_x, rank_y, rank_d = 2 * y + 1 - x, 2 - 2 * y + x, 3 - chaos

    def device(index, rank):
        return {"space": index, "chaos": rank}

    sibling = device(2 * z + 1 - core, chaos)

    def offset(j):
        return (part + (1 + core) * (1 - 2 * j) + space_count) % space_count

    facing = [device(2 * (offset(j) // 2) + core, 2 * y + offset(j) % 2) for j in range(2)]
    barrier = pltpu.get_barrier_semaphore()
    peers = [sibling] + [device(2 * z + k, r) for k in range(2) for r in (rank_x, rank_y)]
    for peer in peers + facing:
        pl.semaphore_signal(
            barrier, inc=1, device_id=peer, device_id_type=pl.DeviceIdType.MESH
        )
    loads = [
        pltpu.make_async_copy(
            far.at[:, i * 128 : i * 128 + 128], mine.at[i, f], local.at[2 * i + f]
        )
        for i in range(pairs)
        for f, far in enumerate((modes_far, heading_far))
    ]
    extras = [
        pltpu.make_async_copy(a, b, near.at[i])
        for i, (a, b) in enumerate(
            [
                (nodes_far, nodes_t), (weights_far, weights), (codes_far, codes),
                (k_far, k_ref), (sensitivity_far, sensitivity), (decay_far, decay),
            ]
        )
    ]
    for load in loads + extras:
        load.start()
    for load in loads:
        load.wait()
    pl.semaphore_wait(barrier, len(peers + facing))

    def span(rank, first, count):
        return field.at[pl.ds(rank * pairs + first, count), :, 0:TERMS]

    firsts = []
    kind = jnp.where(home, 2, 0)
    rank_to = jnp.where(home, rank_y, rank_x)
    for p in range(2):
        for k in range(2):
            at = k * half + p * piece
            i = 2 * p + k
            firsts.append(
                remote(
                    mine.at[at : at + piece], span(chaos, at, piece), first_send.at[i],
                    recv.at[kind + p], device(2 * z + k, rank_to),
                )
            )
    width = half * 128
    heat = [source_far.at[:, k * width : k * width + width] for k in range(2)]
    crossing = [
        remote(
            heat[k], source.at[0], first_send.at[4 + k], first_recv.at[5],
            device(2 * z + k, rank_x),
        )
        for k in range(2)
    ]

    def heat_of(k):
        return source_far.at[:, pl.ds(pl.multiple_of(k * width, 128), width)]

    tables = ((material_far, material), (neighbors_far, neighbors), (picks_far, picks))
    given = [
        remote(a, b, on_send.at[i], first_recv.at[i], sibling)
        for i, (a, b) in enumerate(tables)
    ] + [
        remote(mine, span(chaos, 0, pairs), on_send.at[3], first_recv.at[3], sibling),
        remote(heat_of(1 - core), source.at[1], on_send.at[4], first_recv.at[4], sibling),
    ]
    taken = [
        pltpu.make_async_copy(a, b, on_send.at[5 + i]) for i, (a, b) in enumerate(tables)
    ] + [
        pltpu.make_async_copy(mine, span(chaos, 0, pairs), on_send.at[8]),
        pltpu.make_async_copy(heat_of(core), source.at[1], on_send.at[9]),
    ]

    for copy in firsts:
        copy.start()

    @pl.when(home)
    def _():
        for copy in given + taken:
            copy.start()

    @pl.when(jnp.logical_not(home))
    def _():
        for copy in crossing:
            copy.start()

    for load in extras:
        load.wait()
    fill_tables(nodes_t, weights, codes, left, right, mass)

    @pl.when(home)
    def _():
        for copy in taken:
            copy.wait()

    @pl.when(jnp.logical_not(home))
    def _():
        for copy in given:
            copy.wait_recv()

    fill_aux(k_ref, sensitivity, decay, material, table, field)

    def evaluate_span(start, count):
        def body(i, carry):
            evaluate(field[start + i, 0], field[start + i, 1], start + i, left[...], store)
            return carry

        lax.fori_loop(0, count, body, 0)

    def own_columns(rank, at):
        def body(i, carry):
            columns(2 * (rank * pairs + core * half) + i, 2 * at + i, store, acc)
            return carry

        lax.fori_loop(0, 2 * half, body, 0)

    def region(kind, p, side):
        rank = (rank_x, rank_y, rank_d)[kind]
        return rank, jnp.where(side == 0, core, 1 - core) * half + p * piece

    later = []

    def arrived(kind, p, side):
        ref = span(*region(kind, p, side), piece)
        remote(ref, ref, send.at[0], recv.at[6 * side + 2 * kind + p], sibling).wait_recv()
        return ref

    def hand_on(ref, kind, p, side, target):
        copy = remote(
            ref, ref, send.at[len(later)], recv.at[6 * side + 2 * kind + p], target
        )
        copy.start()
        later.append(copy)

    def take(kind, p):
        ref = arrived(kind, p, 0)
        if kind == 0:
            hand_on(ref, 2, p, 0, device(space, rank_y))
        hand_on(ref, kind, p, 1, sibling)

    def work(kind, p):
        for side in range(2):
            if side == 1:
                arrived(kind, p, 1)
            rank, first = region(kind, p, side)
            evaluate_span(rank * pairs + first, piece)

    evaluate_span(chaos * pairs, pairs)
    take(0, 0)
    take(1, 0)
    work(0, 0)
    own_columns(chaos, half)
    take(0, 1)
    take(1, 1)
    work(1, 0)
    work(0, 1)
    own_columns(rank_x, 0)
    work(1, 1)
    take(2, 0)
    work(2, 0)
    take(2, 1)
    arrived(2, 1, 1)
    halo = []
    for j in range(2):
        pack_halo(picks[0, offset(j)], picks[1, offset(j)], field, out.at[j])
        copy = remote(
            out.at[j], inbox.at[2 * core + j], halo_send.at[j], halo_recv.at[j], facing[j]
        )
        copy.start()
        halo.append(copy)
    for side in range(2):
        rank, first = region(2, 1, side)
        evaluate_span(rank * pairs + first, piece)

    def halo_pair(i):
        evaluate(inbox[i, 0], inbox[i, 1], blocks // 2 + i, left[...], store)

    for j in range(2):
        halo[j].wait_recv()
        ref = inbox.at[2 * core + j]
        copy = remote(ref, ref, halo_send.at[2 + j], halo_recv.at[2 + j], sibling)
        copy.start()
        later.append(copy)
    for j in range(2):
        halo_pair(2 * core + j)
    for j in range(2):
        ref = inbox.at[2 - 2 * core + j]
        remote(ref, ref, halo_send.at[2 + j], halo_recv.at[2 + j], sibling).wait_recv()
        halo_pair(2 - 2 * core + j)

    def result(i):
        return stage.at[i, :, 0:TERMS]

    def place(side, i):
        at = pl.multiple_of((side * half + i) * 128, 128)
        return total.at[:, :, pl.ds(at, 128)]

    def late(rank, at, i):
        faces(rank * pairs + core * half + i, at + i, ranks, halo_depth, neighbors, store, acc, bal)
        sums = project(slice(0, store.shape[3]), right, bal)
        warm = source[at // half, :, pl.ds(pl.multiple_of(i * 128, 128), 128)]
        stage[at + i, 0] = sums[:, 0:128] - mass[...] * warm
        stage[at + i, 1] = sums[:, 128:256]

    def back_across(i):
        return remote(
            result(i), place(core, i), back_send.at[i], back_recv.at[core * half + i],
            device(part, rank_x),
        )

    def back_beside(i):
        return remote(
            result(half + i), place(core, i), back_send.at[half + i],
            back_recv.at[2 * half + i], sibling,
        )

    def back_here(i):
        return pltpu.make_async_copy(
            result(half + i), place(core, i), back_send.at[half + i]
        )

    def far_pair(i, carry):
        late(rank_x, 0, i)
        back_across(i).start()
        return carry

    def near_pair(i, carry):
        late(chaos, half, i)

        @pl.when(home)
        def _():
            back_here(i).start()

        @pl.when(jnp.logical_not(home))
        def _():
            back_beside(i).start()

        return carry

    remote(heat[0], source.at[0], first_send.at[0], first_recv.at[5], sibling).wait_recv()
    lax.fori_loop(0, half, far_pair, 0)
    lax.fori_loop(0, half, near_pair, 0)
    for copy in firsts + later + halo:
        copy.wait_send()
    for i in range(half):
        back_across(i).wait_send()

    @pl.when(home)
    def _():
        for copy in given:
            copy.wait_send()
        for i in range(half):
            back_here(i).wait()
            remote(
                result(half + i), place(1 - core, i), back_send.at[half + i],
                back_recv.at[2 * half + i], sibling,
            ).wait_recv()

    @pl.when(jnp.logical_not(home))
    def _():
        for copy in crossing:
            copy.wait_send()
        for i in range(half):
            back_beside(i).wait_send()
            for k in range(2):
                remote(
                    result(i), place(k, i), back_send.at[i], back_recv.at[k * half + i],
                    sibling,
                ).wait_recv()


def paired_device(
    chaos_modes, newton_heading, source, nodes, weights, k_ref, sensitivity, decay,
    material, neighbors, send_list,
):
    space_count = lax.axis_size("space")
    cells = chaos_modes.shape[1]
    pairs = cells // 128
    half = pairs // 2
    halo_depth = send_list.shape[2]
    queue = nodes.shape[0]
    blocks = material.shape[0]
    far = pl.BlockSpec(memory_space=pltpu.HBM)
    dma = pltpu.SemaphoreType.DMA
    total = pl.pallas_call(
        functools.partial(paired_kernel, (space_count, pairs, halo_depth)),
        out_shape=pltpu.VMEM((2, TERMS, cells), F32),
        in_specs=[far] * 12,
        out_specs=pl.BlockSpec(memory_space=pltpu.VMEM),
        scratch_shapes=[
            pltpu.VMEM((blocks // 2, 2, 88, 128), F32),
            pltpu.VMEM((pairs, 2, TERMS, 128), F32),
            pltpu.VMEM((256, queue), BF),
            pltpu.VMEM((176, queue), BF),
            pltpu.VMEM((88, 1), F32),
            pltpu.VMEM((blocks + 8, 4, SITES, queue), F32),
            pltpu.VMEM((2 * pairs, 2, SITES, queue), F32),
            pltpu.VMEM((2, 256, queue), BF),
            pltpu.VMEM((pairs, 2, 88, 128), F32),
            pltpu.VMEM((2, 1, half * 128), F32),
            pltpu.VMEM((nodes.shape[1], queue), F32),
            pltpu.VMEM((1, queue), F32),
            pltpu.VMEM((8, 128), F32),
            pltpu.VMEM((NMAT, 2, 8, 128), F32),
            pltpu.VMEM((2, 2, 88, 128), F32),
            pltpu.VMEM((4, 2, 88, 128), F32),
            pltpu.SMEM(k_ref.shape, F32),
            pltpu.SMEM(sensitivity.shape, F32),
            pltpu.SMEM(decay.shape, F32),
            pltpu.SMEM((blocks,), jnp.int32),
            pltpu.SMEM((4, blocks), jnp.int32),
            pltpu.SMEM((halo_depth, space_count), jnp.int32),
            dma((2 * pairs,)), dma((6,)), dma((6,)), dma((6,)), dma((10,)), dma((8,)),
            dma((12,)), dma((4,)), dma((4,)), dma((2 * half,)), dma((3 * half,)),
        ],
        compiler_params=pltpu.CompilerParams(
            collective_id=1, has_side_effects=True, vmem_limit_bytes=54 * 1024 * 1024
        ),
    )(
        k_ref, sensitivity, decay, material, neighbors.T, send_list[0].T, chaos_modes,
        newton_heading, nodes.T, weights[None, :], jnp.asarray(order_codes(nodes.shape[1])),
        source[None, :],
    )
    return total[0], total[1]


def device_program(*args):
    modes, nodes, halo_depth = args[0], args[3], args[10].shape[2]
    space_count = lax.axis_size("space")
    paired = lax.axis_size("chaos") == 4 and space_count % 2 == 0 and space_count > 4
    fits = modes.shape[1] % 512 == 0 and nodes.shape[0] <= SPAN and halo_depth == 2
    return (paired_device if paired and fits else per_device)(*args)


def solution(mesh):
    return jax.shard_map(
        device_program,
        mesh=mesh,
        in_specs=(
            P(None, ("space", "chaos")),
            P(None, ("space", "chaos")),
            P(("space", "chaos")),
            P(), P(), P(), P(), P(),
            P("space"),
            P("space", None),
            P("space", None, None),
        ),
        out_specs=(P(None, ("space", "chaos")), P(None, ("space", "chaos"))),
        check_vma=False,
    )
```

```python
import functools
import math

import jax
import jax.numpy as jnp
import numpy as np
from jax import lax
from jax.experimental import pallas as pl
from jax.experimental.pallas import tpu as pltpu
from jax.sharding import PartitionSpec as P

NMAT = 4
SITES = 64
TERMS = 84
MAIN = 80
LOG2E = 1.0 / math.log(2.0)
LN2 = math.log(2.0)
OFFSETS = (1, -1, 2, -2)
SPAN = 512
BF = jnp.bfloat16
F32 = jnp.float32


def compositions(remaining, places):
    if places == 1:
        return [[remaining]]
    listing = []
    for leading in range(remaining, -1, -1):
        for trailing in compositions(remaining - leading, places - 1):
            listing.append([leading] + trailing)
    return listing


def chaos_orders(variables):
    listing = []
    for degree in range(4):
        listing = listing + compositions(degree, variables)
    return np.array(listing, dtype=np.int32)


def half_turn(x, wanted):
    return jnp.where(wanted, pltpu.roll(x, 64, 1), x)


def factors(x, o):
    second = (x * x - 1.0) * np.float32(1.0 / math.sqrt(2.0))
    third = (x * x * x - 3.0 * x) * np.float32(1.0 / math.sqrt(6.0))
    return jnp.where(o == 0, 1.0, jnp.where(o == 1, x, jnp.where(o == 2, second, third)))


def order_codes(dims):
    orders = chaos_orders(dims)
    code = (orders * 4 ** np.arange(dims)[None, :]).sum(1)
    out = np.zeros((8, 128), np.float32)
    out[0, :TERMS] = code
    return out


def upright(row):
    return jnp.transpose(jnp.broadcast_to(row, (128, 128)))


def stacked(main, tail, lower):
    row = lax.broadcasted_iota(jnp.int32, tail.shape, 0)
    high = main.astype(BF)
    low = (main - high.astype(F32)).astype(BF)
    tail_high = tail.astype(BF).astype(F32)
    tail_low = tail - tail_high
    if lower:
        parts = [high, high, low]
        ends = [jnp.where(row < 4, tail_high, pltpu.roll(tail_high, 4, 0)), tail_low]
    else:
        parts = [high, low, high]
        ends = [jnp.where(row < 4, tail_high, pltpu.roll(tail_low, 4, 0)), tail_high]
    ends[1] = jnp.where(row < 4, ends[1], 0.0)
    return jnp.concatenate(parts + [jnp.concatenate(ends, 0).astype(BF)], 0)


def fill_tables(nodes_t, weights, codes, left, right, mass):
    dims = nodes_t.shape[0]
    code = upright(codes[0:1, 0:128])[0:88].astype(jnp.int32)
    row = lax.broadcasted_iota(jnp.int32, (88, 1), 0)
    mass[...] = jnp.zeros(mass.shape, F32)

    def body(part, carry):
        span = pl.ds(pl.multiple_of(part * 128, 128), 128)
        value = jnp.ones((88, 128), F32)
        for d in range(dims):
            value = value * factors(nodes_t[d : d + 1, span], (code // 4**d) % 4)
        value = jnp.where(row < TERMS, value, 0.0)
        left[:, span] = stacked(value[0:80], value[80:88], True)
        value = value * weights[:, span]
        mass[...] += jnp.sum(value, axis=1, keepdims=True)
        value = value * 0.25
        high = value.astype(BF).astype(F32)
        right[:, span] = jnp.concatenate([high, value - high], 0).astype(BF)
        return carry

    lax.fori_loop(0, nodes_t.shape[1] // 128, body, 0)


def fill_aux(k_ref, sensitivity, decay, material, table, field):
    row = lax.broadcasted_iota(jnp.int32, (8, 128), 0)
    low_half = lax.broadcasted_iota(jnp.int32, (8, 128), 1) < 64
    dims = sensitivity.shape[1]
    for m in range(NMAT):
        tile = jnp.log(jnp.full((8, 128), k_ref[m], F32))
        for d in range(dims):
            tile = jnp.where(row == d + 1, sensitivity[m, d], tile)
        tile = jnp.where(row == 7, -decay[m], tile) * np.float32(LOG2E)
        table[m, 0] = pltpu.roll(tile, 4, 0)
        table[m, 1] = tile
    for i in range(material.shape[0] // 2):
        a, b = material[2 * i], material[2 * i + 1]
        for f in range(2):
            field[i, f, 84:88] = jnp.where(low_half, table[a, f], table[b, f])[4:8]


def remote(src, dst, send, recv, device):
    return pltpu.make_async_remote_copy(
        src_ref=src, dst_ref=dst, send_sem=send, recv_sem=recv,
        device_id=device, device_id_type=pl.DeviceIdType.MESH,
    )


def greet(space_count, chaos_count, space, chaos):
    barrier = pltpu.get_barrier_semaphore()
    peers = [(chaos + k) % chaos_count for k in range(1, chaos_count)]
    for peer in peers:
        pl.semaphore_signal(
            barrier, inc=1, device_id={"chaos": peer}, device_id_type=pl.DeviceIdType.MESH
        )
    for offset in OFFSETS:
        pl.semaphore_signal(
            barrier, inc=1, device_id={"space": (space + offset + space_count) % space_count},
            device_id_type=pl.DeviceIdType.MESH,
        )
    return barrier, peers


def evaluate(m, h, index, basis, store):
    row = lax.broadcasted_iota(jnp.int32, (8, 128), 0)
    aux = jnp.where(row < 4, pltpu.roll(m[80:88], 4, 0), h[80:88])
    damp = aux[7:8]
    arg = m * damp
    first = arg[0:8] + jnp.where(row < 7, aux, 0.0)
    rate = jnp.transpose(jnp.broadcast_to(damp * np.float32(LN2), (128, 128)))
    sides = [
        jnp.transpose(stacked(x, y, False))
        for x, y in (
            (m[0:80], m[80:88]), (h[0:80], h[80:88]),
            (jnp.concatenate([first, arg[8:80]], 0), arg[80:88]),
        )
    ]
    rows = [s[16 * c : 16 * c + 16] for c in range(8) for s in sides]
    r = jnp.dot(jnp.concatenate(rows, 0), basis, preferred_element_type=F32)
    for c in range(8):
        t = r[48 * c : 48 * c + 16]
        dt = r[48 * c + 16 : 48 * c + 32]
        k = jnp.exp2(r[48 * c + 32 : 48 * c + 48])
        speed = rate[16 * c : 16 * c + 16]
        dk = k * (dt * jnp.concatenate([speed] * (dt.shape[1] // 128), 1))
        block = 2 * index + c // 4
        at = slice(16 * (c % 4), 16 * (c % 4) + 16)
        store[block, 0, at] = t
        store[block, 1, at] = dt
        store[block, 2, at] = k
        store[block, 3, at] = dk


def columns(block, index, store, acc):
    width = 128
    shape = (SITES, width)
    row = lax.broadcasted_iota(jnp.int32, shape, 0)
    top = row == SITES - 1
    bottom = row == 0
    for part in range(store.shape[3] // width):
        at = slice(part * width, part * width + width)
        t, dt, k, dk = [store[block, f, :, at] for f in range(4)]
        up = [pltpu.roll(x, SITES - 1, 0) for x in (t, dt, k, dk)]
        gap = jnp.where(top, 0.0, t - up[0])
        step = jnp.where(top, 0.0, dt - up[1])
        both = k + up[2]
        change = dk + up[3]
        flow = both * gap
        turn = change * gap + both * step
        below = jnp.where(bottom, -4.0 * k * t, pltpu.roll(flow, 1, 0))
        under = jnp.where(bottom, -4.0 * (k * dt + dk * t), pltpu.roll(turn, 1, 0))
        acc[index, 0, :, at] = 2.0 * (flow - below)
        acc[index, 1, :, at] = 2.0 * (turn - under)


def pack_halo(e0, e1, field, out):
    low_half = lax.broadcasted_iota(jnp.int32, (1, 128), 1) < 64
    for f in range(2):
        x0 = half_turn(field[e0 // 2, f], e0 % 2 == 1)
        x1 = half_turn(field[e1 // 2, f], e1 % 2 == 0)
        out[f] = jnp.where(low_half, x0, x1)


def send_halo(space_count, space, picks, field, out, inbox, send, recv):
    copies = []
    for i, offset in enumerate(OFFSETS):
        target = (space + offset + space_count) % space_count
        pack_halo(picks[0, target], picks[1, target], field, out.at[i])
        copy = remote(out.at[i], inbox.at[i], send.at[i], recv.at[i], {"space": target})
        copy.start()
        copies.append(copy)
    return copies


def slot(neighbors, own, block, face, ranks, halo_depth):
    space, space_count, blocks = ranks
    entry = neighbors[face, block]
    away = jnp.maximum(entry - blocks, 0)
    distance = (space - away // halo_depth + space_count) % space_count
    order = jnp.where(
        distance == 1, 0, jnp.where(distance == space_count - 1, 1, jnp.where(distance == 2, 2, 3))
    )
    index = jnp.where(
        entry >= blocks, blocks + order * halo_depth + away % halo_depth, entry
    )
    return jnp.where(entry >= 0, index, own)


def faces(pair, local, ranks, halo_depth, neighbors, store, acc, bal):
    for j in range(2):
        own = 2 * pair + j
        mine = 2 * local + j
        others = [slot(neighbors, own, own, f, ranks, halo_depth) for f in range(4)]
        for c in range(SITES // 16):
            rows = slice(16 * c, 16 * c + 16)
            for part in range(store.shape[3] // 128):
                at = slice(part * 128, part * 128 + 128)
                t, dt, k, dk = [store[own, f, rows, at] for f in range(4)]
                flow = acc[mine, 0, rows, at]
                turn = acc[mine, 1, rows, at]
                for e in others:
                    gap = t - store[e, 0, rows, at]
                    step = dt - store[e, 1, rows, at]
                    both = k + store[e, 2, rows, at]
                    change = dk + store[e, 3, rows, at]
                    flow += both * gap
                    turn += change * gap + both * step
                for side, x in ((0, flow), (1, turn)):
                    high = x.astype(BF)
                    spot = slice(128 * side + 64 * j + 16 * c, 128 * side + 64 * j + 16 * c + 16)
                    bal[0, spot, at] = high
                    bal[1, spot, at] = (x - high.astype(F32)).astype(BF)


def project(nodes_at, right, bal):
    turned = (((1,), (1,)), ((), ()))
    one = lax.dot_general(right[:, nodes_at], bal[0], turned, preferred_element_type=F32)
    two = lax.dot_general(right[0:88, nodes_at], bal[1], turned, preferred_element_type=F32)
    return one[0:88] + one[88:176] + two


def keep(total, pair, first, mass, source, res, jvp):
    cols = pl.ds(pl.multiple_of(pair * 128, 128), 128)
    if first:
        res[:, cols] = (total[:, 0:128] - mass[...] * source[:, cols])[0:TERMS]
        jvp[:, cols] = total[0:TERMS, 128:256]
    else:
        res[:, cols] += total[0:TERMS, 0:128]
        jvp[:, cols] += total[0:TERMS, 128:256]


def whole_kernel(
    sizes, picks, k_ref, sensitivity, decay, material, neighbors, modes_far, heading_far,
    nodes_far, weights_far, codes_far, source, res, jvp,
    field, left, right, mass, store, acc, bal,
    nodes_t, weights, codes, table, out, inbox,
    send, recv, halo_send, halo_recv, near, local,
):
    space_count, chaos_count, pairs, halo_depth = sizes
    space = lax.axis_index("space")
    chaos = lax.axis_index("chaos")
    blocks = material.shape[0]
    base = chaos * pairs
    ranks = (space, space_count, blocks)
    barrier, peers = greet(space_count, chaos_count, space, chaos)
    loads = [
        pltpu.make_async_copy(
            far.at[:, i * 128 : i * 128 + 128], field.at[base + i, f, 0:TERMS],
            local.at[2 * i + f],
        )
        for i in range(pairs)
        for f, far in enumerate((modes_far, heading_far))
    ]
    extras = [
        pltpu.make_async_copy(a, b, near.at[i])
        for i, (a, b) in enumerate(
            [(nodes_far, nodes_t), (weights_far, weights), (codes_far, codes)]
        )
    ]
    for load in loads + extras:
        load.start()
    for load in loads:
        load.wait()
    pl.semaphore_wait(barrier, len(peers) + len(OFFSETS))

    def block(owner, first, count):
        return field.at[pl.ds(owner * pairs + first, count), :, 0:TERMS]

    def passing(i, owner, first, count, target):
        ref = block(owner, first, count)
        return remote(ref, ref, send.at[i], recv.at[i], {"chaos": target})

    width = store.shape[3]

    def evaluate_span(start, count, nodes_at=slice(0, width)):
        def body(i, carry):
            evaluate(
                field[start + i, 0], field[start + i, 1], start + i, left[:, nodes_at], store
            )
            return carry

        lax.fori_loop(0, count, body, 0)

    def own_columns():
        def body(i, carry):
            columns(2 * base + i, i, store, acc)
            return carry

        lax.fori_loop(0, 2 * pairs, body, 0)

    def finish(nodes_at, first):
        def late(pair, carry):
            faces(base + pair, pair, ranks, halo_depth, neighbors, store, acc, bal)
            keep(project(nodes_at, right, bal), pair, first, mass, source, res, jvp)
            return carry

        lax.fori_loop(0, pairs, late, 0)

    def mine():
        fill_aux(k_ref, sensitivity, decay, material, table, field)
        for load in extras:
            load.wait()
        fill_tables(nodes_t, weights, codes, left, right, mass)
        evaluate_span(base, pairs)
        own_columns()

    copies = [passing(i, chaos, 0, pairs, t) for i, t in enumerate(peers)]
    for copy in copies:
        copy.start()
    mine()
    for i, copy in enumerate(copies):
        copy.wait_recv()
    halo = send_halo(space_count, space, picks, field, out, inbox, halo_send, halo_recv)
    for i in range(1, chaos_count):
        evaluate_span(((chaos + i) % chaos_count) * pairs, pairs)
    for i, copy in enumerate(halo):
        copy.wait_recv()
        evaluate(inbox[i, 0], inbox[i, 1], blocks // 2 + i, left[:, 0:width], store)
    finish(slice(0, width), True)

    def again(part, carry):
        nodes_at = pl.ds(pl.multiple_of(part * width, width), width)
        evaluate_span(0, blocks // 2, nodes_at)
        for i in range(len(OFFSETS)):
            evaluate(inbox[i, 0], inbox[i, 1], blocks // 2 + i, left[:, nodes_at], store)
        own_columns()
        finish(nodes_at, False)
        return carry

    if left.shape[1] > width:
        lax.fori_loop(1, left.shape[1] // width, again, 0)
    for copy in copies + halo:
        copy.wait_send()


def per_device(
    chaos_modes, newton_heading, source, nodes, weights, k_ref, sensitivity, decay,
    material, neighbors, send_list,
):
    space_count = lax.axis_size("space")
    cells = chaos_modes.shape[1]
    pairs = cells // 128
    halo_depth = send_list.shape[2]
    queue = nodes.shape[0]
    span = min(queue, SPAN)
    blocks = material.shape[0]
    far = pl.BlockSpec(memory_space=pltpu.HBM)
    vmem = pl.BlockSpec(memory_space=pltpu.VMEM)
    smem = pl.BlockSpec(memory_space=pltpu.SMEM)
    return pl.pallas_call(
        functools.partial(
            whole_kernel, (space_count, lax.axis_size("chaos"), pairs, halo_depth)
        ),
        out_shape=[jax.ShapeDtypeStruct((TERMS, cells), F32)] * 2,
        in_specs=[smem] * 6 + [far] * 5 + [vmem],
        out_specs=[vmem] * 2,
        scratch_shapes=[
            pltpu.VMEM((blocks // 2, 2, 88, 128), F32),
            pltpu.VMEM((256, queue), BF),
            pltpu.VMEM((176, queue), BF),
            pltpu.VMEM((88, 1), F32),
            pltpu.VMEM((blocks + 8, 4, SITES, span), F32),
            pltpu.VMEM((2 * pairs, 2, SITES, span), F32),
            pltpu.VMEM((2, 256, span), BF),
            pltpu.VMEM((nodes.shape[1], queue), F32),
            pltpu.VMEM((1, queue), F32),
            pltpu.VMEM((8, 128), F32),
            pltpu.VMEM((NMAT, 2, 8, 128), F32),
            pltpu.VMEM((4, 2, 88, 128), F32),
            pltpu.VMEM((4, 2, 88, 128), F32),
            pltpu.SemaphoreType.DMA((16,)),
            pltpu.SemaphoreType.DMA((16,)),
            pltpu.SemaphoreType.DMA((4,)),
            pltpu.SemaphoreType.DMA((4,)),
            pltpu.SemaphoreType.DMA((3,)),
            pltpu.SemaphoreType.DMA((2 * pairs,)),
        ],
        compiler_params=pltpu.CompilerParams(
            collective_id=0, has_side_effects=True, vmem_limit_bytes=60 * 1024 * 1024
        ),
    )(
        send_list[0].T, k_ref, sensitivity, decay, material, neighbors.T, chaos_modes,
        newton_heading, nodes.T, weights[None, :], jnp.asarray(order_codes(nodes.shape[1])),
        source[None, :],
    )


def paired_kernel(
    sizes, k_far, sensitivity_far, decay_far, material_far, neighbors_far, picks_far, modes_far,
    heading_far, nodes_far, weights_far, codes_far, source_far, total,
    field, mine, left, right, mass, store, acc, bal, stage, source,
    nodes_t, weights, codes, table, out, inbox, k_ref, sensitivity, decay, material,
    neighbors, picks,
    local, near, first_send, first_recv, on_send, send, recv, halo_send, halo_recv,
    back_send, back_recv,
):
    space_count, pairs, halo_depth = sizes
    space = lax.axis_index("space")
    chaos = lax.axis_index("chaos")
    z, core = space // 2, space % 2
    y, x = chaos // 2, chaos % 2
    home = core == x
    part = 2 * z + x
    half, piece = pairs // 2, pairs // 4
    blocks = material.shape[0]
    ranks = (part, space_count, blocks)
    rank_x, rank_y, rank_d = 2 * y + 1 - x, 2 - 2 * y + x, 3 - chaos

    def device(index, rank):
        return {"space": index, "chaos": rank}

    sibling = device(2 * z + 1 - core, chaos)

    def offset(j):
        return (part + (1 + core) * (1 - 2 * j) + space_count) % space_count

    facing = [device(2 * (offset(j) // 2) + core, 2 * y + offset(j) % 2) for j in range(2)]
    barrier = pltpu.get_barrier_semaphore()
    peers = [sibling] + [device(2 * z + k, r) for k in range(2) for r in (rank_x, rank_y)]
    for peer in peers + facing:
        pl.semaphore_signal(
            barrier, inc=1, device_id=peer, device_id_type=pl.DeviceIdType.MESH
        )
    loads = [
        pltpu.make_async_copy(
            far.at[:, i * 128 : i * 128 + 128], mine.at[i, f], local.at[2 * i + f]
        )
        for i in range(pairs)
        for f, far in enumerate((modes_far, heading_far))
    ]
    extras = [
        pltpu.make_async_copy(a, b, near.at[i])
        for i, (a, b) in enumerate(
            [
                (nodes_far, nodes_t), (weights_far, weights), (codes_far, codes),
                (k_far, k_ref), (sensitivity_far, sensitivity), (decay_far, decay),
            ]
        )
    ]
    for load in loads + extras:
        load.start()
    for load in loads:
        load.wait()
    pl.semaphore_wait(barrier, len(peers + facing))

    def span(rank, first, count):
        return field.at[pl.ds(rank * pairs + first, count), :, 0:TERMS]

    firsts = []
    kind = jnp.where(home, 2, 0)
    rank_to = jnp.where(home, rank_y, rank_x)
    for p in range(2):
        for k in range(2):
            at = k * half + p * piece
            i = 2 * p + k
            firsts.append(
                remote(
                    mine.at[at : at + piece], span(chaos, at, piece), first_send.at[i],
                    recv.at[kind + p], device(2 * z + k, rank_to),
                )
            )
    width = half * 128
    heat = [source_far.at[:, k * width : k * width + width] for k in range(2)]
    crossing = [
        remote(
            heat[k], source.at[0], first_send.at[4 + k], first_recv.at[5],
            device(2 * z + k, rank_x),
        )
        for k in range(2)
    ]

    def heat_of(k):
        return source_far.at[:, pl.ds(pl.multiple_of(k * width, 128), width)]

    tables = ((material_far, material), (neighbors_far, neighbors), (picks_far, picks))
    given = [
        remote(a, b, on_send.at[i], first_recv.at[i], sibling)
        for i, (a, b) in enumerate(tables)
    ] + [
        remote(mine, span(chaos, 0, pairs), on_send.at[3], first_recv.at[3], sibling),
        remote(heat_of(1 - core), source.at[1], on_send.at[4], first_recv.at[4], sibling),
    ]
    taken = [
        pltpu.make_async_copy(a, b, on_send.at[5 + i]) for i, (a, b) in enumerate(tables)
    ] + [
        pltpu.make_async_copy(mine, span(chaos, 0, pairs), on_send.at[8]),
        pltpu.make_async_copy(heat_of(core), source.at[1], on_send.at[9]),
    ]

    for copy in firsts:
        copy.start()

    @pl.when(home)
    def _():
        for copy in given + taken:
            copy.start()

    @pl.when(jnp.logical_not(home))
    def _():
        for copy in crossing:
            copy.start()

    for load in extras:
        load.wait()
    fill_tables(nodes_t, weights, codes, left, right, mass)

    @pl.when(home)
    def _():
        for copy in taken:
            copy.wait()

    @pl.when(jnp.logical_not(home))
    def _():
        for copy in given:
            copy.wait_recv()

    fill_aux(k_ref, sensitivity, decay, material, table, field)

    def evaluate_span(start, count):
        def body(i, carry):
            evaluate(field[start + i, 0], field[start + i, 1], start + i, left[...], store)
            return carry

        lax.fori_loop(0, count, body, 0)

    def own_columns(rank, at):
        def body(i, carry):
            columns(2 * (rank * pairs + core * half) + i, 2 * at + i, store, acc)
            return carry

        lax.fori_loop(0, 2 * half, body, 0)

    def region(kind, p, side):
        rank = (rank_x, rank_y, rank_d)[kind]
        return rank, jnp.where(side == 0, core, 1 - core) * half + p * piece

    later = []

    def arrived(kind, p, side):
        ref = span(*region(kind, p, side), piece)
        remote(ref, ref, send.at[0], recv.at[6 * side + 2 * kind + p], sibling).wait_recv()
        return ref

    def hand_on(ref, kind, p, side, target):
        copy = remote(
            ref, ref, send.at[len(later)], recv.at[6 * side + 2 * kind + p], target
        )
        copy.start()
        later.append(copy)

    def take(kind, p):
        ref = arrived(kind, p, 0)
        if kind == 0:
            hand_on(ref, 2, p, 0, device(space, rank_y))
        hand_on(ref, kind, p, 1, sibling)

    def work(kind, p, wait):
        for side in range(2):
            if side == 1 and wait:
                arrived(kind, p, 1)
            rank, first = region(kind, p, side)
            evaluate_span(rank * pairs + first, piece)

    evaluate_span(chaos * pairs, pairs)
    take(0, 0)
    take(1, 0)
    work(0, 0, True)
    own_columns(chaos, half)
    take(0, 1)
    take(1, 1)
    work(1, 0, True)
    work(0, 1, True)
    work(1, 1, True)
    take(2, 0)
    take(2, 1)
    arrived(2, 0, 1)
    arrived(2, 1, 1)
    halo = []
    for j in range(2):
        pack_halo(picks[0, offset(j)], picks[1, offset(j)], field, out.at[j])
        copy = remote(
            out.at[j], inbox.at[2 * core + j], halo_send.at[j], halo_recv.at[j], facing[j]
        )
        copy.start()
        halo.append(copy)
    work(2, 0, False)
    work(2, 1, False)
    own_columns(rank_x, 0)

    def halo_pair(i):
        evaluate(inbox[i, 0], inbox[i, 1], blocks // 2 + i, left[...], store)

    for j in range(2):
        halo[j].wait_recv()
        ref = inbox.at[2 * core + j]
        copy = remote(ref, ref, halo_send.at[2 + j], halo_recv.at[2 + j], sibling)
        copy.start()
        later.append(copy)
    for j in range(2):
        halo_pair(2 * core + j)
    for j in range(2):
        ref = inbox.at[2 - 2 * core + j]
        remote(ref, ref, halo_send.at[2 + j], halo_recv.at[2 + j], sibling).wait_recv()
        halo_pair(2 - 2 * core + j)

    def result(i):
        return stage.at[i, :, 0:TERMS]

    def place(side, i):
        at = pl.multiple_of((side * half + i) * 128, 128)
        return total.at[:, :, pl.ds(at, 128)]

    def late(rank, at, i):
        faces(rank * pairs + core * half + i, at + i, ranks, halo_depth, neighbors, store, acc, bal)
        sums = project(slice(0, store.shape[3]), right, bal)
        warm = source[at // half, :, pl.ds(pl.multiple_of(i * 128, 128), 128)]
        stage[at + i, 0] = sums[:, 0:128] - mass[...] * warm
        stage[at + i, 1] = sums[:, 128:256]

    def back_across(i):
        return remote(
            result(i), place(core, i), back_send.at[i], back_recv.at[core * half + i],
            device(part, rank_x),
        )

    def back_beside(i):
        return remote(
            result(half + i), place(core, i), back_send.at[half + i],
            back_recv.at[2 * half + i], sibling,
        )

    def back_here(i):
        return pltpu.make_async_copy(
            result(half + i), place(core, i), back_send.at[half + i]
        )

    def far_pair(i, carry):
        late(rank_x, 0, i)
        back_across(i).start()
        return carry

    def near_pair(i, carry):
        late(chaos, half, i)

        @pl.when(home)
        def _():
            back_here(i).start()

        @pl.when(jnp.logical_not(home))
        def _():
            back_beside(i).start()

        return carry

    remote(heat[0], source.at[0], first_send.at[0], first_recv.at[5], sibling).wait_recv()
    lax.fori_loop(0, half, far_pair, 0)
    lax.fori_loop(0, half, near_pair, 0)
    for copy in firsts + later + halo:
        copy.wait_send()
    for i in range(half):
        back_across(i).wait_send()

    @pl.when(home)
    def _():
        for copy in given:
            copy.wait_send()
        for i in range(half):
            back_here(i).wait()
            remote(
                result(half + i), place(1 - core, i), back_send.at[half + i],
                back_recv.at[2 * half + i], sibling,
            ).wait_recv()

    @pl.when(jnp.logical_not(home))
    def _():
        for copy in crossing:
            copy.wait_send()
        for i in range(half):
            back_beside(i).wait_send()
            for k in range(2):
                remote(
                    result(i), place(k, i), back_send.at[i], back_recv.at[k * half + i],
                    sibling,
                ).wait_recv()


def paired_device(
    chaos_modes, newton_heading, source, nodes, weights, k_ref, sensitivity, decay,
    material, neighbors, send_list,
):
    space_count = lax.axis_size("space")
    cells = chaos_modes.shape[1]
    pairs = cells // 128
    half = pairs // 2
    halo_depth = send_list.shape[2]
    queue = nodes.shape[0]
    blocks = material.shape[0]
    far = pl.BlockSpec(memory_space=pltpu.HBM)
    dma = pltpu.SemaphoreType.DMA
    total = pl.pallas_call(
        functools.partial(paired_kernel, (space_count, pairs, halo_depth)),
        out_shape=pltpu.VMEM((2, TERMS, cells), F32),
        in_specs=[far] * 12,
        out_specs=pl.BlockSpec(memory_space=pltpu.VMEM),
        scratch_shapes=[
            pltpu.VMEM((blocks // 2, 2, 88, 128), F32),
            pltpu.VMEM((pairs, 2, TERMS, 128), F32),
            pltpu.VMEM((256, queue), BF),
            pltpu.VMEM((176, queue), BF),
            pltpu.VMEM((88, 1), F32),
            pltpu.VMEM((blocks + 8, 4, SITES, queue), F32),
            pltpu.VMEM((2 * pairs, 2, SITES, queue), F32),
            pltpu.VMEM((2, 256, queue), BF),
            pltpu.VMEM((pairs, 2, 88, 128), F32),
            pltpu.VMEM((2, 1, half * 128), F32),
            pltpu.VMEM((nodes.shape[1], queue), F32),
            pltpu.VMEM((1, queue), F32),
            pltpu.VMEM((8, 128), F32),
            pltpu.VMEM((NMAT, 2, 8, 128), F32),
            pltpu.VMEM((2, 2, 88, 128), F32),
            pltpu.VMEM((4, 2, 88, 128), F32),
            pltpu.SMEM(k_ref.shape, F32),
            pltpu.SMEM(sensitivity.shape, F32),
            pltpu.SMEM(decay.shape, F32),
            pltpu.SMEM((blocks,), jnp.int32),
            pltpu.SMEM((4, blocks), jnp.int32),
            pltpu.SMEM((halo_depth, space_count), jnp.int32),
            dma((2 * pairs,)), dma((6,)), dma((6,)), dma((6,)), dma((10,)), dma((8,)),
            dma((12,)), dma((4,)), dma((4,)), dma((2 * half,)), dma((3 * half,)),
        ],
        compiler_params=pltpu.CompilerParams(
            collective_id=1, has_side_effects=True, vmem_limit_bytes=54 * 1024 * 1024
        ),
    )(
        k_ref, sensitivity, decay, material, neighbors.T, send_list[0].T, chaos_modes,
        newton_heading, nodes.T, weights[None, :], jnp.asarray(order_codes(nodes.shape[1])),
        source[None, :],
    )
    return total[0], total[1]


def device_program(*args):
    modes, nodes, halo_depth = args[0], args[3], args[10].shape[2]
    space_count = lax.axis_size("space")
    paired = lax.axis_size("chaos") == 4 and space_count % 2 == 0 and space_count > 4
    fits = modes.shape[1] % 512 == 0 and nodes.shape[0] <= SPAN and halo_depth == 2
    return (paired_device if paired and fits else per_device)(*args)


def solution(mesh):
    return jax.shard_map(
        device_program,
        mesh=mesh,
        in_specs=(
            P(None, ("space", "chaos")),
            P(None, ("space", "chaos")),
            P(("space", "chaos")),
            P(), P(), P(), P(), P(),
            P("space"),
            P("space", None),
            P("space", None, None),
        ),
        out_specs=(P(None, ("space", "chaos")), P(None, ("space", "chaos"))),
        check_vma=False,
    )
```

```python
import functools
import math

import jax
import jax.numpy as jnp
import numpy as np
from jax import lax
from jax.experimental import pallas as pl
from jax.experimental.pallas import tpu as pltpu
from jax.sharding import PartitionSpec as P

NMAT = 4
SITES = 64
TERMS = 84
MAIN = 80
LOG2E = 1.0 / math.log(2.0)
LN2 = math.log(2.0)
OFFSETS = (1, -1, 2, -2)
SPAN = 512
BF = jnp.bfloat16
F32 = jnp.float32


def compositions(remaining, places):
    if places == 1:
        return [[remaining]]
    listing = []
    for leading in range(remaining, -1, -1):
        for trailing in compositions(remaining - leading, places - 1):
            listing.append([leading] + trailing)
    return listing


def chaos_orders(variables):
    listing = []
    for degree in range(4):
        listing = listing + compositions(degree, variables)
    return np.array(listing, dtype=np.int32)


def half_turn(x, wanted):
    return jnp.where(wanted, pltpu.roll(x, 64, 1), x)


def factors(x, o):
    second = (x * x - 1.0) * np.float32(1.0 / math.sqrt(2.0))
    third = (x * x * x - 3.0 * x) * np.float32(1.0 / math.sqrt(6.0))
    return jnp.where(o == 0, 1.0, jnp.where(o == 1, x, jnp.where(o == 2, second, third)))


def order_codes(dims):
    orders = chaos_orders(dims)
    code = (orders * 4 ** np.arange(dims)[None, :]).sum(1)
    out = np.zeros((8, 128), np.float32)
    out[0, :TERMS] = code
    return out


def upright(row):
    return jnp.transpose(jnp.broadcast_to(row, (128, 128)))


def stacked(main, tail, lower):
    row = lax.broadcasted_iota(jnp.int32, tail.shape, 0)
    high = main.astype(BF)
    low = (main - high.astype(F32)).astype(BF)
    tail_high = tail.astype(BF).astype(F32)
    tail_low = tail - tail_high
    if lower:
        parts = [high, high, low]
        ends = [jnp.where(row < 4, tail_high, pltpu.roll(tail_high, 4, 0)), tail_low]
    else:
        parts = [high, low, high]
        ends = [jnp.where(row < 4, tail_high, pltpu.roll(tail_low, 4, 0)), tail_high]
    ends[1] = jnp.where(row < 4, ends[1], 0.0)
    return jnp.concatenate(parts + [jnp.concatenate(ends, 0).astype(BF)], 0)


def fill_tables(nodes_t, weights, codes, left, right, mass):
    dims = nodes_t.shape[0]
    code = upright(codes[0:1, 0:128])[0:88].astype(jnp.int32)
    row = lax.broadcasted_iota(jnp.int32, (88, 1), 0)
    mass[...] = jnp.zeros(mass.shape, F32)

    def body(part, carry):
        span = pl.ds(pl.multiple_of(part * 128, 128), 128)
        value = jnp.ones((88, 128), F32)
        for d in range(dims):
            value = value * factors(nodes_t[d : d + 1, span], (code // 4**d) % 4)
        value = jnp.where(row < TERMS, value, 0.0)
        left[:, span] = stacked(value[0:80], value[80:88], True)
        value = value * weights[:, span]
        mass[...] += jnp.sum(value, axis=1, keepdims=True)
        value = value * 0.25
        high = value.astype(BF).astype(F32)
        right[:, span] = jnp.concatenate([high, value - high], 0).astype(BF)
        return carry

    lax.fori_loop(0, nodes_t.shape[1] // 128, body, 0)


def fill_aux(k_ref, sensitivity, decay, material, table, field):
    row = lax.broadcasted_iota(jnp.int32, (8, 128), 0)
    low_half = lax.broadcasted_iota(jnp.int32, (8, 128), 1) < 64
    dims = sensitivity.shape[1]
    for m in range(NMAT):
        tile = jnp.log(jnp.full((8, 128), k_ref[m], F32))
        for d in range(dims):
            tile = jnp.where(row == d + 1, sensitivity[m, d], tile)
        tile = jnp.where(row == 7, -decay[m], tile) * np.float32(LOG2E)
        table[m, 0] = pltpu.roll(tile, 4, 0)
        table[m, 1] = tile
    for i in range(material.shape[0] // 2):
        a, b = material[2 * i], material[2 * i + 1]
        for f in range(2):
            field[i, f, 84:88] = jnp.where(low_half, table[a, f], table[b, f])[4:8]


def remote(src, dst, send, recv, device):
    return pltpu.make_async_remote_copy(
        src_ref=src, dst_ref=dst, send_sem=send, recv_sem=recv,
        device_id=device, device_id_type=pl.DeviceIdType.MESH,
    )


def greet(space_count, chaos_count, space, chaos):
    barrier = pltpu.get_barrier_semaphore()
    peers = [(chaos + k) % chaos_count for k in range(1, chaos_count)]
    for peer in peers:
        pl.semaphore_signal(
            barrier, inc=1, device_id={"chaos": peer}, device_id_type=pl.DeviceIdType.MESH
        )
    for offset in OFFSETS:
        pl.semaphore_signal(
            barrier, inc=1, device_id={"space": (space + offset + space_count) % space_count},
            device_id_type=pl.DeviceIdType.MESH,
        )
    return barrier, peers


def evaluate(m, h, index, basis, store):
    row = lax.broadcasted_iota(jnp.int32, (8, 128), 0)
    aux = jnp.where(row < 4, pltpu.roll(m[80:88], 4, 0), h[80:88])
    damp = aux[7:8]
    arg = m * damp
    first = arg[0:8] + jnp.where(row < 7, aux, 0.0)
    rate = jnp.transpose(jnp.broadcast_to(damp * np.float32(LN2), (128, 128)))
    sides = [
        jnp.transpose(stacked(x, y, False))
        for x, y in (
            (m[0:80], m[80:88]), (h[0:80], h[80:88]),
            (jnp.concatenate([first, arg[8:80]], 0), arg[80:88]),
        )
    ]
    rows = [s[16 * c : 16 * c + 16] for c in range(8) for s in sides]
    r = jnp.dot(jnp.concatenate(rows, 0), basis, preferred_element_type=F32)
    for c in range(8):
        t = r[48 * c : 48 * c + 16]
        dt = r[48 * c + 16 : 48 * c + 32]
        k = jnp.exp2(r[48 * c + 32 : 48 * c + 48])
        speed = rate[16 * c : 16 * c + 16]
        dk = k * (dt * jnp.concatenate([speed] * (dt.shape[1] // 128), 1))
        block = 2 * index + c // 4
        at = slice(16 * (c % 4), 16 * (c % 4) + 16)
        store[block, 0, at] = t
        store[block, 1, at] = dt
        store[block, 2, at] = k
        store[block, 3, at] = dk


def columns(block, index, store, acc):
    width = 128
    shape = (SITES, width)
    row = lax.broadcasted_iota(jnp.int32, shape, 0)
    top = row == SITES - 1
    bottom = row == 0
    for part in range(store.shape[3] // width):
        at = slice(part * width, part * width + width)
        t, dt, k, dk = [store[block, f, :, at] for f in range(4)]
        up = [pltpu.roll(x, SITES - 1, 0) for x in (t, dt, k, dk)]
        gap = jnp.where(top, 0.0, t - up[0])
        step = jnp.where(top, 0.0, dt - up[1])
        both = k + up[2]
        change = dk + up[3]
        flow = both * gap
        turn = change * gap + both * step
        below = jnp.where(bottom, -4.0 * k * t, pltpu.roll(flow, 1, 0))
        under = jnp.where(bottom, -4.0 * (k * dt + dk * t), pltpu.roll(turn, 1, 0))
        acc[index, 0, :, at] = 2.0 * (flow - below)
        acc[index, 1, :, at] = 2.0 * (turn - under)


def pack_halo(e0, e1, field, out):
    low_half = lax.broadcasted_iota(jnp.int32, (1, 128), 1) < 64
    for f in range(2):
        x0 = half_turn(field[e0 // 2, f], e0 % 2 == 1)
        x1 = half_turn(field[e1 // 2, f], e1 % 2 == 0)
        out[f] = jnp.where(low_half, x0, x1)


def send_halo(space_count, space, picks, field, out, inbox, send, recv):
    copies = []
    for i, offset in enumerate(OFFSETS):
        target = (space + offset + space_count) % space_count
        pack_halo(picks[0, target], picks[1, target], field, out.at[i])
        copy = remote(out.at[i], inbox.at[i], send.at[i], recv.at[i], {"space": target})
        copy.start()
        copies.append(copy)
    return copies


def slot(neighbors, own, block, face, ranks, halo_depth):
    space, space_count, blocks = ranks
    entry = neighbors[face, block]
    away = jnp.maximum(entry - blocks, 0)
    distance = (space - away // halo_depth + space_count) % space_count
    order = jnp.where(
        distance == 1, 0, jnp.where(distance == space_count - 1, 1, jnp.where(distance == 2, 2, 3))
    )
    index = jnp.where(
        entry >= blocks, blocks + order * halo_depth + away % halo_depth, entry
    )
    return jnp.where(entry >= 0, index, own)


def faces(pair, local, ranks, halo_depth, neighbors, store, acc, bal):
    for j in range(2):
        own = 2 * pair + j
        mine = 2 * local + j
        others = [slot(neighbors, own, own, f, ranks, halo_depth) for f in range(4)]
        for c in range(SITES // 16):
            rows = slice(16 * c, 16 * c + 16)
            for part in range(store.shape[3] // 256):
                at = slice(part * 256, part * 256 + 256)
                t, dt, k, dk = [store[own, f, rows, at] for f in range(4)]
                flow = acc[mine, 0, rows, at]
                turn = acc[mine, 1, rows, at]
                for e in others:
                    gap = t - store[e, 0, rows, at]
                    step = dt - store[e, 1, rows, at]
                    both = k + store[e, 2, rows, at]
                    change = dk + store[e, 3, rows, at]
                    flow += both * gap
                    turn += change * gap + both * step
                for side, x in ((0, flow), (1, turn)):
                    high = x.astype(BF)
                    spot = slice(128 * side + 64 * j + 16 * c, 128 * side + 64 * j + 16 * c + 16)
                    bal[0, spot, at] = high
                    bal[1, spot, at] = (x - high.astype(F32)).astype(BF)


def project(nodes_at, right, bal):
    turned = (((1,), (1,)), ((), ()))
    one = lax.dot_general(right[:, nodes_at], bal[0], turned, preferred_element_type=F32)
    two = lax.dot_general(right[0:88, nodes_at], bal[1], turned, preferred_element_type=F32)
    return one[0:88] + one[88:176] + two


def keep(total, pair, first, mass, source, res, jvp):
    cols = pl.ds(pl.multiple_of(pair * 128, 128), 128)
    if first:
        res[:, cols] = (total[:, 0:128] - mass[...] * source[:, cols])[0:TERMS]
        jvp[:, cols] = total[0:TERMS, 128:256]
    else:
        res[:, cols] += total[0:TERMS, 0:128]
        jvp[:, cols] += total[0:TERMS, 128:256]


def whole_kernel(
    sizes, picks, k_ref, sensitivity, decay, material, neighbors, modes_far, heading_far,
    nodes_far, weights_far, codes_far, source, res, jvp,
    field, left, right, mass, store, acc, bal,
    nodes_t, weights, codes, table, out, inbox,
    send, recv, halo_send, halo_recv, near, local,
):
    space_count, chaos_count, pairs, halo_depth = sizes
    space = lax.axis_index("space")
    chaos = lax.axis_index("chaos")
    blocks = material.shape[0]
    base = chaos * pairs
    ranks = (space, space_count, blocks)
    barrier, peers = greet(space_count, chaos_count, space, chaos)
    loads = [
        pltpu.make_async_copy(
            far.at[:, i * 128 : i * 128 + 128], field.at[base + i, f, 0:TERMS],
            local.at[2 * i + f],
        )
        for i in range(pairs)
        for f, far in enumerate((modes_far, heading_far))
    ]
    extras = [
        pltpu.make_async_copy(a, b, near.at[i])
        for i, (a, b) in enumerate(
            [(nodes_far, nodes_t), (weights_far, weights), (codes_far, codes)]
        )
    ]
    for load in loads + extras:
        load.start()
    for load in loads:
        load.wait()
    pl.semaphore_wait(barrier, len(peers) + len(OFFSETS))

    def block(owner, first, count):
        return field.at[pl.ds(owner * pairs + first, count), :, 0:TERMS]

    def passing(i, owner, first, count, target):
        ref = block(owner, first, count)
        return remote(ref, ref, send.at[i], recv.at[i], {"chaos": target})

    width = store.shape[3]

    def evaluate_span(start, count, nodes_at=slice(0, width)):
        def body(i, carry):
            evaluate(
                field[start + i, 0], field[start + i, 1], start + i, left[:, nodes_at], store
            )
            return carry

        lax.fori_loop(0, count, body, 0)

    def own_columns():
        def body(i, carry):
            columns(2 * base + i, i, store, acc)
            return carry

        lax.fori_loop(0, 2 * pairs, body, 0)

    def finish(nodes_at, first):
        def late(pair, carry):
            faces(base + pair, pair, ranks, halo_depth, neighbors, store, acc, bal)
            keep(project(nodes_at, right, bal), pair, first, mass, source, res, jvp)
            return carry

        lax.fori_loop(0, pairs, late, 0)

    def mine():
        fill_aux(k_ref, sensitivity, decay, material, table, field)
        for load in extras:
            load.wait()
        fill_tables(nodes_t, weights, codes, left, right, mass)
        evaluate_span(base, pairs)
        own_columns()

    copies = [passing(i, chaos, 0, pairs, t) for i, t in enumerate(peers)]
    for copy in copies:
        copy.start()
    mine()
    for i, copy in enumerate(copies):
        copy.wait_recv()
    halo = send_halo(space_count, space, picks, field, out, inbox, halo_send, halo_recv)
    for i in range(1, chaos_count):
        evaluate_span(((chaos + i) % chaos_count) * pairs, pairs)
    for i, copy in enumerate(halo):
        copy.wait_recv()
        evaluate(inbox[i, 0], inbox[i, 1], blocks // 2 + i, left[:, 0:width], store)
    finish(slice(0, width), True)

    def again(part, carry):
        nodes_at = pl.ds(pl.multiple_of(part * width, width), width)
        evaluate_span(0, blocks // 2, nodes_at)
        for i in range(len(OFFSETS)):
            evaluate(inbox[i, 0], inbox[i, 1], blocks // 2 + i, left[:, nodes_at], store)
        own_columns()
        finish(nodes_at, False)
        return carry

    if left.shape[1] > width:
        lax.fori_loop(1, left.shape[1] // width, again, 0)
    for copy in copies + halo:
        copy.wait_send()


def per_device(
    chaos_modes, newton_heading, source, nodes, weights, k_ref, sensitivity, decay,
    material, neighbors, send_list,
):
    space_count = lax.axis_size("space")
    cells = chaos_modes.shape[1]
    pairs = cells // 128
    halo_depth = send_list.shape[2]
    queue = nodes.shape[0]
    span = min(queue, SPAN)
    blocks = material.shape[0]
    far = pl.BlockSpec(memory_space=pltpu.HBM)
    vmem = pl.BlockSpec(memory_space=pltpu.VMEM)
    smem = pl.BlockSpec(memory_space=pltpu.SMEM)
    return pl.pallas_call(
        functools.partial(
            whole_kernel, (space_count, lax.axis_size("chaos"), pairs, halo_depth)
        ),
        out_shape=[jax.ShapeDtypeStruct((TERMS, cells), F32)] * 2,
        in_specs=[smem] * 6 + [far] * 5 + [vmem],
        out_specs=[vmem] * 2,
        scratch_shapes=[
            pltpu.VMEM((blocks // 2, 2, 88, 128), F32),
            pltpu.VMEM((256, queue), BF),
            pltpu.VMEM((176, queue), BF),
            pltpu.VMEM((88, 1), F32),
            pltpu.VMEM((blocks + 8, 4, SITES, span), F32),
            pltpu.VMEM((2 * pairs, 2, SITES, span), F32),
            pltpu.VMEM((2, 256, span), BF),
            pltpu.VMEM((nodes.shape[1], queue), F32),
            pltpu.VMEM((1, queue), F32),
            pltpu.VMEM((8, 128), F32),
            pltpu.VMEM((NMAT, 2, 8, 128), F32),
            pltpu.VMEM((4, 2, 88, 128), F32),
            pltpu.VMEM((4, 2, 88, 128), F32),
            pltpu.SemaphoreType.DMA((16,)),
            pltpu.SemaphoreType.DMA((16,)),
            pltpu.SemaphoreType.DMA((4,)),
            pltpu.SemaphoreType.DMA((4,)),
            pltpu.SemaphoreType.DMA((3,)),
            pltpu.SemaphoreType.DMA((2 * pairs,)),
        ],
        compiler_params=pltpu.CompilerParams(
            collective_id=0, has_side_effects=True, vmem_limit_bytes=60 * 1024 * 1024
        ),
    )(
        send_list[0].T, k_ref, sensitivity, decay, material, neighbors.T, chaos_modes,
        newton_heading, nodes.T, weights[None, :], jnp.asarray(order_codes(nodes.shape[1])),
        source[None, :],
    )


def paired_kernel(
    sizes, k_far, sensitivity_far, decay_far, material_far, neighbors_far, picks_far, modes_far,
    heading_far, nodes_far, weights_far, codes_far, source_far, total,
    field, mine, left, right, mass, store, acc, bal, stage, source,
    nodes_t, weights, codes, table, out, inbox, k_ref, sensitivity, decay, material,
    neighbors, picks,
    local, near, first_send, first_recv, on_send, send, recv, halo_send, halo_recv,
    back_send, back_recv,
):
    space_count, pairs, halo_depth = sizes
    space = lax.axis_index("space")
    chaos = lax.axis_index("chaos")
    z, core = space // 2, space % 2
    y, x = chaos // 2, chaos % 2
    home = core == x
    part = 2 * z + x
    half = pairs // 2
    piece = (half - half // 4, half // 4)
    head = (0, piece[0])
    blocks = material.shape[0]
    ranks = (part, space_count, blocks)
    rank_x, rank_y, rank_d = 2 * y + 1 - x, 2 - 2 * y + x, 3 - chaos

    def device(index, rank):
        return {"space": index, "chaos": rank}

    sibling = device(2 * z + 1 - core, chaos)

    def offset(j):
        return (part + (1 + core) * (1 - 2 * j) + space_count) % space_count

    facing = [device(2 * (offset(j) // 2) + core, 2 * y + offset(j) % 2) for j in range(2)]
    barrier = pltpu.get_barrier_semaphore()
    peers = [sibling] + [device(2 * z + k, r) for k in range(2) for r in (rank_x, rank_y)]
    for peer in peers + facing:
        pl.semaphore_signal(
            barrier, inc=1, device_id=peer, device_id_type=pl.DeviceIdType.MESH
        )
    loads = [
        pltpu.make_async_copy(
            far.at[:, i * 128 : i * 128 + 128], mine.at[i, f], local.at[2 * i + f]
        )
        for i in range(pairs)
        for f, far in enumerate((modes_far, heading_far))
    ]
    extras = [
        pltpu.make_async_copy(a, b, near.at[i])
        for i, (a, b) in enumerate(
            [
                (nodes_far, nodes_t), (weights_far, weights), (codes_far, codes),
                (k_far, k_ref), (sensitivity_far, sensitivity), (decay_far, decay),
            ]
        )
    ]
    for load in loads + extras:
        load.start()
    for load in loads:
        load.wait()
    pl.semaphore_wait(barrier, len(peers + facing))

    def span(rank, first, count):
        return field.at[pl.ds(rank * pairs + first, count), :, 0:TERMS]

    firsts = []
    kind = jnp.where(home, 2, 0)
    rank_to = jnp.where(home, rank_y, rank_x)
    for p in range(2):
        for k in range(2):
            at = k * half + head[p]
            i = 2 * p + k
            firsts.append(
                remote(
                    mine.at[at : at + piece[p]], span(chaos, at, piece[p]), first_send.at[i],
                    recv.at[kind + p], device(2 * z + k, rank_to),
                )
            )
    width = half * 128
    heat = [source_far.at[:, k * width : k * width + width] for k in range(2)]
    crossing = [
        remote(
            heat[k], source.at[0], first_send.at[4 + k], first_recv.at[5],
            device(2 * z + k, rank_x),
        )
        for k in range(2)
    ]

    def heat_of(k):
        return source_far.at[:, pl.ds(pl.multiple_of(k * width, 128), width)]

    tables = ((material_far, material), (neighbors_far, neighbors), (picks_far, picks))
    given = [
        remote(a, b, on_send.at[i], first_recv.at[i], sibling)
        for i, (a, b) in enumerate(tables)
    ] + [
        remote(mine, span(chaos, 0, pairs), on_send.at[3], first_recv.at[3], sibling),
        remote(heat_of(1 - core), source.at[1], on_send.at[4], first_recv.at[4], sibling),
    ]
    taken = [
        pltpu.make_async_copy(a, b, on_send.at[5 + i]) for i, (a, b) in enumerate(tables)
    ] + [
        pltpu.make_async_copy(mine, span(chaos, 0, pairs), on_send.at[8]),
        pltpu.make_async_copy(heat_of(core), source.at[1], on_send.at[9]),
    ]

    for copy in firsts:
        copy.start()

    @pl.when(home)
    def _():
        for copy in given + taken:
            copy.start()

    @pl.when(jnp.logical_not(home))
    def _():
        for copy in crossing:
            copy.start()

    for load in extras:
        load.wait()
    fill_tables(nodes_t, weights, codes, left, right, mass)

    @pl.when(home)
    def _():
        for copy in taken:
            copy.wait()

    @pl.when(jnp.logical_not(home))
    def _():
        for copy in given:
            copy.wait_recv()

    fill_aux(k_ref, sensitivity, decay, material, table, field)

    def evaluate_span(start, count):
        def body(i, carry):
            evaluate(field[start + i, 0], field[start + i, 1], start + i, left[...], store)
            return carry

        lax.fori_loop(0, count, body, 0)

    def own_columns(rank, at):
        def body(i, carry):
            columns(2 * (rank * pairs + core * half) + i, 2 * at + i, store, acc)
            return carry

        lax.fori_loop(0, 2 * half, body, 0)

    def region(kind, p, side):
        rank = (rank_x, rank_y, rank_d)[kind]
        return rank, jnp.where(side == 0, core, 1 - core) * half + head[p]

    later = []

    def arrived(kind, p, side):
        ref = span(*region(kind, p, side), piece[p])
        remote(ref, ref, send.at[0], recv.at[6 * side + 2 * kind + p], sibling).wait_recv()
        return ref

    def hand_on(ref, kind, p, side, target):
        copy = remote(
            ref, ref, send.at[len(later)], recv.at[6 * side + 2 * kind + p], target
        )
        copy.start()
        later.append(copy)

    def take(kind, p):
        ref = arrived(kind, p, 0)
        if kind == 0:
            hand_on(ref, 2, p, 0, device(space, rank_y))
        hand_on(ref, kind, p, 1, sibling)

    def work(kind, p, wait):
        for side in range(2):
            if side == 1 and wait:
                arrived(kind, p, 1)
            rank, first = region(kind, p, side)
            evaluate_span(rank * pairs + first, piece[p])

    evaluate_span(chaos * pairs, pairs)
    take(0, 0)
    take(1, 0)
    work(0, 0, True)
    own_columns(chaos, half)
    take(0, 1)
    take(1, 1)
    work(1, 0, True)
    work(0, 1, True)
    work(1, 1, True)
    take(2, 0)
    take(2, 1)
    arrived(2, 0, 1)
    arrived(2, 1, 1)
    halo = []
    for j in range(2):
        pack_halo(picks[0, offset(j)], picks[1, offset(j)], field, out.at[j])
        copy = remote(
            out.at[j], inbox.at[2 * core + j], halo_send.at[j], halo_recv.at[j], facing[j]
        )
        copy.start()
        halo.append(copy)
    work(2, 0, False)
    work(2, 1, False)
    own_columns(rank_x, 0)

    def halo_pair(i):
        evaluate(inbox[i, 0], inbox[i, 1], blocks // 2 + i, left[...], store)

    for j in range(2):
        halo[j].wait_recv()
        ref = inbox.at[2 * core + j]
        copy = remote(ref, ref, halo_send.at[2 + j], halo_recv.at[2 + j], sibling)
        copy.start()
        later.append(copy)
    for j in range(2):
        halo_pair(2 * core + j)
    for j in range(2):
        ref = inbox.at[2 - 2 * core + j]
        remote(ref, ref, halo_send.at[2 + j], halo_recv.at[2 + j], sibling).wait_recv()
        halo_pair(2 - 2 * core + j)

    def result(i):
        return stage.at[i, :, 0:TERMS]

    def place(side, i):
        at = pl.multiple_of((side * half + i) * 128, 128)
        return total.at[:, :, pl.ds(at, 128)]

    def late(rank, at, i):
        faces(rank * pairs + core * half + i, at + i, ranks, halo_depth, neighbors, store, acc, bal)
        sums = project(slice(0, store.shape[3]), right, bal)
        warm = source[at // half, :, pl.ds(pl.multiple_of(i * 128, 128), 128)]
        stage[at + i, 0] = sums[:, 0:128] - mass[...] * warm
        stage[at + i, 1] = sums[:, 128:256]

    def back_across(i):
        return remote(
            result(i), place(core, i), back_send.at[i], back_recv.at[core * half + i],
            device(part, rank_x),
        )

    def back_beside(i):
        return remote(
            result(half + i), place(core, i), back_send.at[half + i],
            back_recv.at[2 * half + i], sibling,
        )

    def back_here(i):
        return pltpu.make_async_copy(
            result(half + i), place(core, i), back_send.at[half + i]
        )

    def far_pair(i, carry):
        late(rank_x, 0, i)
        back_across(i).start()
        return carry

    def near_pair(i, carry):
        late(chaos, half, i)

        @pl.when(home)
        def _():
            back_here(i).start()

        @pl.when(jnp.logical_not(home))
        def _():
            back_beside(i).start()

        return carry

    remote(heat[0], source.at[0], first_send.at[0], first_recv.at[5], sibling).wait_recv()
    lax.fori_loop(0, half, far_pair, 0)
    lax.fori_loop(0, half, near_pair, 0)
    for copy in firsts + later + halo:
        copy.wait_send()
    for i in range(half):
        back_across(i).wait_send()

    @pl.when(home)
    def _():
        for copy in given:
            copy.wait_send()
        for i in range(half):
            back_here(i).wait()
            remote(
                result(half + i), place(1 - core, i), back_send.at[half + i],
                back_recv.at[2 * half + i], sibling,
            ).wait_recv()

    @pl.when(jnp.logical_not(home))
    def _():
        for copy in crossing:
            copy.wait_send()
        for i in range(half):
            back_beside(i).wait_send()
            for k in range(2):
                remote(
                    result(i), place(k, i), back_send.at[i], back_recv.at[k * half + i],
                    sibling,
                ).wait_recv()


def paired_device(
    chaos_modes, newton_heading, source, nodes, weights, k_ref, sensitivity, decay,
    material, neighbors, send_list,
):
    space_count = lax.axis_size("space")
    cells = chaos_modes.shape[1]
    pairs = cells // 128
    half = pairs // 2
    halo_depth = send_list.shape[2]
    queue = nodes.shape[0]
    blocks = material.shape[0]
    far = pl.BlockSpec(memory_space=pltpu.HBM)
    dma = pltpu.SemaphoreType.DMA
    total = pl.pallas_call(
        functools.partial(paired_kernel, (space_count, pairs, halo_depth)),
        out_shape=pltpu.VMEM((2, TERMS, cells), F32),
        in_specs=[far] * 12,
        out_specs=pl.BlockSpec(memory_space=pltpu.VMEM),
        scratch_shapes=[
            pltpu.VMEM((blocks // 2, 2, 88, 128), F32),
            pltpu.VMEM((pairs, 2, TERMS, 128), F32),
            pltpu.VMEM((256, queue), BF),
            pltpu.VMEM((176, queue), BF),
            pltpu.VMEM((88, 1), F32),
            pltpu.VMEM((blocks + 8, 4, SITES, queue), F32),
            pltpu.VMEM((2 * pairs, 2, SITES, queue), F32),
            pltpu.VMEM((2, 256, queue), BF),
            pltpu.VMEM((pairs, 2, 88, 128), F32),
            pltpu.VMEM((2, 1, half * 128), F32),
            pltpu.VMEM((nodes.shape[1], queue), F32),
            pltpu.VMEM((1, queue), F32),
            pltpu.VMEM((8, 128), F32),
            pltpu.VMEM((NMAT, 2, 8, 128), F32),
            pltpu.VMEM((2, 2, 88, 128), F32),
            pltpu.VMEM((4, 2, 88, 128), F32),
            pltpu.SMEM(k_ref.shape, F32),
            pltpu.SMEM(sensitivity.shape, F32),
            pltpu.SMEM(decay.shape, F32),
            pltpu.SMEM((blocks,), jnp.int32),
            pltpu.SMEM((4, blocks), jnp.int32),
            pltpu.SMEM((halo_depth, space_count), jnp.int32),
            dma((2 * pairs,)), dma((6,)), dma((6,)), dma((6,)), dma((10,)), dma((8,)),
            dma((12,)), dma((4,)), dma((4,)), dma((2 * half,)), dma((3 * half,)),
        ],
        compiler_params=pltpu.CompilerParams(
            collective_id=1, has_side_effects=True, vmem_limit_bytes=54 * 1024 * 1024
        ),
    )(
        k_ref, sensitivity, decay, material, neighbors.T, send_list[0].T, chaos_modes,
        newton_heading, nodes.T, weights[None, :], jnp.asarray(order_codes(nodes.shape[1])),
        source[None, :],
    )
    return total[0], total[1]


def device_program(*args):
    modes, nodes, halo_depth = args[0], args[3], args[10].shape[2]
    space_count = lax.axis_size("space")
    paired = lax.axis_size("chaos") == 4 and space_count % 2 == 0 and space_count > 4
    fits = modes.shape[1] % 512 == 0 and nodes.shape[0] <= SPAN and halo_depth == 2
    return (paired_device if paired and fits else per_device)(*args)


def solution(mesh):
    return jax.shard_map(
        device_program,
        mesh=mesh,
        in_specs=(
            P(None, ("space", "chaos")),
            P(None, ("space", "chaos")),
            P(("space", "chaos")),
            P(), P(), P(), P(), P(),
            P("space"),
            P("space", None),
            P("space", None, None),
        ),
        out_specs=(P(None, ("space", "chaos")), P(None, ("space", "chaos"))),
        check_vma=False,
    )
```
